256 devices in a mesh: path: 64 (over y, z, core), inner: 4 (over x).
Axes of the slice: x: 4, y: 4, z: 8, core: 2. Of those that a mesh axis runs over, the one named last changes fastest.
Arguments:
- acts: bfloat16 [65536, 2048], P(('path', 'inner')), may hold values from -6 to 6
- cotan: bfloat16 [65536, 2048], P(('path', 'inner')), may hold values from -6 to 6
- w_in: bfloat16 [64, 2048, 2048], P('path', None, 'inner'), may hold values from -0.125 to 0.125
- w_out_t: bfloat16 [64, 2048, 2048], P('path', None, 'inner'), may hold values from -0.125 to 0.125
- choose: int32 [64, 2], replicated, may hold values from 0 to 7
- momentum: float32 [2, 8, 2048, 2048], P(None, None, 'path', 'inner'), may hold values from -6 to 6
Outputs:
- new_in: bfloat16 [64, 2048, 2048], P('path', None, 'inner')
- new_out_t: bfloat16 [64, 2048, 2048], P('path', None, 'inner')
- new_momentum: float32 [2, 8, 2048, 2048], P(None, None, 'path', 'inner')
The draws below stay inside these ranges and needn't reach their ends.
All inputs are finite; a program needn't handle non-finite values. Where the reference program divides by a largest or mean magnitude, that divisor is 1e-20 or more.
Results may differ from the reference program's by a relative error of at most 0.015.
Values may be sent and summed in bfloat16 or wider, within the bound.
A program may use at most 128 MiB of HBM per device.

```python
import math
import jax
import jax.numpy as jnp
import numpy as np
from jax import lax

D = 2048
GRID = 8
LEVELS = 2
BLOCK = 128
TOK_DEV = 256
PATHS = 64
TOKENS = 65536
N_INNER = 4


def place_ends(entries, own_key, least, high):
    longest = entries.shape.index(max(entries.shape))
    spots = []
    for shift in (0, 1):
        where = [jax.random.randint(jax.random.fold_in(own_key, axis), (), 0, length) for axis, length in enumerate(entries.shape)]
        where[longest] = (where[longest] + shift) % entries.shape[longest]
        spots.append(tuple(where))
    return entries.at[spots[0]].set(least).at[spots[1]].set(high)


def block_scale(stream_key, dims, cuts, smallest, top_value):
    factor_of, own = 1.0, jax.random.fold_in(stream_key, 6)
    for dim, parts in cuts:
        steps = jnp.exp(jax.random.uniform(jax.random.fold_in(own, dim), (parts,), jnp.float32, smallest / len(cuts), top_value / len(cuts)))
        factor_of = factor_of * jnp.repeat(steps, dims[dim] // parts).reshape([-1 if axis == dim else 1 for axis in range(len(dims))])
    return factor_of


def rank_table(count, slope):
    weights = [(1 << 20) // math.isqrt(standing ** slope) + 1 for standing in range(1, count + 1)]
    deviation = 1 + sum(weights) // (1 << 30)
    return np.cumsum(np.array([max(1, weight // deviation) for weight in weights]))


def ranked(rng, extent, number_of, lean):
    listing = rank_table(number_of, lean)
    ticket = jax.random.randint(jax.random.fold_in(rng, 1), extent, 0, int(listing[number_of - 1]))
    standing = jnp.searchsorted(jnp.asarray(listing, jnp.int32), ticket, side="right")
    return jax.random.permutation(jax.random.fold_in(rng, 2), number_of)[standing].astype(jnp.int32)


def noise(rng, shape, deviation, bound, shards=(), held_as=jnp.bfloat16):
    entries = jax.random.normal(rng, shape, jnp.float32) * deviation
    if len(shards) > 0:
        entries = block_scale(rng, shape, shards, -0.22, 0.18) * entries
    return jnp.clip(entries, min=-bound, max=bound).astype(held_as)


def setup_inputs(seed: int = 0) -> dict:
    keys = jax.random.split(jax.random.key(seed), 7)
    acts = noise(keys[0], (TOKENS, D), 1.0, 6.0, ((0, 256),))
    cotan = noise(keys[1], (TOKENS, D), 1.0, 6.0, ((0, 256),))
    w_in = noise(keys[2], (PATHS, D, D), D ** -0.5, 0.125, ((0, 64), (2, 4)))
    w_out_t = noise(keys[3], (PATHS, D, D), D ** -0.5, 0.125, ((0, 64), (2, 4)))
    choose = place_ends(ranked(keys[4], (PATHS, LEVELS), GRID, 2), jax.random.fold_in(keys[4], 3), 0, GRID - 1).astype(jnp.int32)
    momentum = noise(keys[5], (LEVELS, GRID, D, D), 0.5, 6.0, ((2, 64), (3, 4)), jnp.float32)
    return dict(acts=acts, cotan=cotan, w_in=w_in, w_out_t=w_out_t, choose=choose, momentum=momentum)


EPS = 1e-06
MU = 0.9
OUTER_LR = 0.7

def quantize(values):
    shape = values.shape
    blocks = values.reshape(shape[:-1] + (shape[-1] // BLOCK, BLOCK))
    scale = lax.optimization_barrier(jnp.max(jnp.abs(blocks), axis=-1)) + EPS
    code = (blocks / scale[..., None]).astype(jnp.bfloat16).reshape(shape)
    return (code, scale)

def dequantize(code, scale):
    shape = code.shape
    blocks = code.astype(jnp.float32).reshape(shape[:-1] + (shape[-1] // BLOCK, BLOCK))
    return (blocks * scale[..., None]).reshape(shape)

def reference(acts, cotan, w_in, w_out_t, choose, momentum):
    tok_path = TOK_DEV * N_INNER
    norm = 1.0 / jnp.sqrt(jnp.float32(tok_path))
    inputs = acts.reshape(PATHS, tok_path, D)
    cotans = cotan.reshape(PATHS, tok_path, D)

    def inner_step(items):
        x_rows, c_rows, first, second = items
        pre = jnp.dot(x_rows, first, preferred_element_type=jnp.float32)
        tanh_val = jnp.tanh(pre)
        tanh_low = tanh_val.astype(jnp.bfloat16)
        grad_out = jnp.dot(c_rows.T, tanh_low, preferred_element_type=jnp.float32) * norm
        back = jnp.dot(c_rows, second, preferred_element_type=jnp.float32)
        dsum = (back * (1.0 - tanh_val * tanh_val)).astype(jnp.bfloat16)
        grad_in = jnp.dot(x_rows.T, dsum, preferred_element_type=jnp.float32) * norm
        code_in, scale_in = quantize(grad_in)
        code_out, scale_out = quantize(grad_out)
        return (code_in, scale_in, code_out, scale_out)
    code_in, scale_in, code_out, scale_out = lax.map(inner_step, (inputs, cotans, w_in, w_out_t))

    def owner(codes, scales, ids, mom):

        def add(carry, item):
            total, count = carry
            code, scale, module = item
            total = total.at[module].add(dequantize(code, scale))
            count = count + (jnp.arange(GRID) == module).astype(jnp.float32)
            return ((total, count), None)
        start = (jnp.zeros((GRID, D, D), jnp.float32), jnp.zeros((GRID,), jnp.float32))
        (total, count), _ = lax.scan(add, start, (codes, scales, ids))
        avg = total / jnp.maximum(count, 1.0)[:, None, None]
        new_mom = MU * mom + avg
        update = MU * new_mom + avg
        ucode, uscale = quantize(update)
        return (new_mom, ucode, uscale)
    mom_in, ucode_in, uscale_in = owner(code_in, scale_in, choose[:, 0], momentum[0])
    mom_out, ucode_out, uscale_out = owner(code_out, scale_out, choose[:, 1], momentum[1])

    def apply(items):
        weight, module, ucode, uscale = items
        return (weight.astype(jnp.float32) - OUTER_LR * dequantize(ucode[module], uscale[module])).astype(jnp.bfloat16)
    new_in = lax.map(lambda items: apply((items[0], items[1], ucode_in, uscale_in)), (w_in, choose[:, 0]))
    new_out_t = lax.map(lambda items: apply((items[0], items[1], ucode_out, uscale_out)), (w_out_t, choose[:, 1]))
    return (new_in, new_out_t, jnp.stack([mom_in, mom_out]))
```

```python
import functools

import jax
import jax.numpy as jnp
from jax import lax
from jax.experimental import pallas as pl
from jax.experimental.pallas import tpu as pltpu
from jax.sharding import PartitionSpec as P

MU = 0.9
OUTER_LR = 0.7
MESH = pl.DeviceIdType.MESH

NX, NY, NZ, NC = 4, 4, 8, 2
GRID = 8
TOK = 256
TOKENS = TOK * NX
D = 2048
COLS = D // NX
PIECE = D // (NY * NZ * NC)
NPAIR = NZ // 2
PAIR = 2 * NC * PIECE
CHUNK = NY * PAIR
PEERS = [(2, 0), (2, 1), (1, 0), (1, 1), (3, 0), (3, 1), (0, 1)]
NP = len(PEERS)
ORDER = [2, 1, 3, 0]
HOPS = [4, 3, 2, 1, -3, -2, -1]


def contract_first(left, right):
    return lax.dot_general(
        left, right, (((0,), (0,)), ((), ())), preferred_element_type=jnp.float32
    )


class Body:
    def __init__(self, ins, outs, scratch):
        self.x_hbm, self.c_hbm, self.w1_hbm, self.w2_hbm, self.ch, self.chv, self.mom_hbm = ins
        self.f_hbm = outs[:2]
        self.nm_hbm = outs[2]
        for name, ref in scratch.items():
            setattr(self, name, ref)
        path = lax.axis_index("path")
        self.x = lax.axis_index("inner")
        self.y = lax.div(path, NZ * NC)
        self.z = lax.rem(lax.div(path, NC), NZ)
        self.c = lax.rem(path, NC)
        self.zp = lax.div(self.z, 2)

    def path_of(self, dy=0, dz=0, dc=0):
        y = lax.rem(self.y + (dy + NY), NY)
        z = lax.rem(self.z + (dz + NZ), NZ)
        c = lax.rem(self.c + (dc + NC), NC)
        return (y * NZ + z) * NC + c

    def dev(self, dy=0, dz=0, dc=0, dx=0):
        return (self.path_of(dy, dz, dc), lax.rem(self.x + (dx + NX), NX))

    def send(self, src, dst, ssem, rsem, dev):
        pltpu.make_async_remote_copy(
            src_ref=src, dst_ref=dst, send_sem=ssem, recv_sem=rsem, device_id=dev, device_id_type=MESH
        ).start()

    def wait(self, ref, sem):
        pltpu.make_async_copy(ref, ref, sem).wait()

    def barrier(self):
        bar = pltpu.get_barrier_semaphore()
        partners = [self.dev(dx=k) for k in (1, 2, 3)]
        partners += [self.dev(dy=dy, dc=dc) for dy, dc in PEERS]
        partners += [self.dev(dz=1), self.dev(dz=-1)]
        for partner in partners:
            pl.semaphore_signal(bar, inc=1, device_id=partner, device_id_type=MESH)
        pl.semaphore_wait(bar, len(partners))

    def pair(self, i):
        return lax.rem(self.zp + ORDER[i], NPAIR)

    def load_local(self):
        for a, (hbm, whbm, wbuf) in enumerate(
            ((self.x_hbm, self.w1_hbm, self.W1), (self.c_hbm, self.w2_hbm, self.W2))
        ):
            for i in range(NPAIR):
                q = self.pair(i)

                def one(yy, _, a=a, i=i, q=q, hbm=hbm, whbm=whbm, wbuf=wbuf):
                    cols = pl.multiple_of(yy * (NPAIR * PAIR) + q * PAIR, PAIR)
                    place = pl.multiple_of(yy * PAIR, PAIR)
                    pltpu.make_async_copy(
                        hbm.at[:, pl.ds(cols, PAIR)],
                        self.T2[a].at[q, pl.ds(pl.multiple_of(self.x * TOK, TOK), TOK), pl.ds(place, PAIR)],
                        self.lsem.at[a, i],
                    ).start()
                    pltpu.make_async_copy(
                        whbm.at[pl.ds(cols, PAIR)], wbuf.at[q, pl.ds(place, PAIR)], self.lsem.at[a, i]
                    ).start()
                    return 0

                lax.fori_loop(0, NY, one, 0)
        pltpu.make_async_copy(self.mom_hbm, self.MOM, self.msem.at[0]).start()

    def send_tokens(self, a, i):
        hbm = (self.x_hbm, self.c_hbm)[a]
        q = self.pair(i)

        def one(yy, _):
            cols = pl.multiple_of(yy * (NPAIR * PAIR) + q * PAIR, PAIR)
            place = pl.multiple_of(yy * PAIR, PAIR)
            for dx in (2, 1, 3):
                self.send(
                    hbm.at[:, pl.ds(cols, PAIR)],
                    self.T2[a].at[q, pl.ds(pl.multiple_of(self.x * TOK, TOK), TOK), pl.ds(place, PAIR)],
                    self.tssem.at[a],
                    self.trsem.at[a, i],
                    self.dev(dx=dx),
                )
            return 0

        lax.fori_loop(0, NY, one, 0)

    def wait_tokens(self, a, i):
        q = self.pair(i)
        wbuf = (self.W1, self.W2)[a]
        self.wait(self.T2[a].at[q, pl.ds(0, TOK)], self.lsem.at[a, i])
        self.wait(wbuf.at[q], self.lsem.at[a, i])
        self.wait(self.T2[a].at[q, pl.ds(0, TOKENS - TOK)], self.trsem.at[a, i])

    def product(self, a, i):
        q = self.pair(i)
        wbuf = (self.W1, self.W2)[a]

        def one(h, _):
            rows = pl.ds(pl.multiple_of(h * 512, 512), 512)
            part = jnp.dot(self.T2[a][q, rows], wbuf[q], preferred_element_type=jnp.float32)
            if i == 0:
                self.ACC[rows] = part
            else:
                self.ACC[rows] = self.ACC[rows] + part
            return 0

        lax.fori_loop(0, TOKENS // 512, one, 0)

    def activate(self):
        def one(h, _):
            rows = pl.ds(pl.multiple_of(h * 64, 64), 64)
            t = jnp.tanh(self.ACC[rows])
            self.TB[rows] = t.astype(jnp.bfloat16)
            self.SL[rows] = 1.0 - t * t
            return 0

        lax.fori_loop(0, TOKENS // 64, one, 0)

    def slope(self):
        def one(h, _):
            rows = pl.ds(pl.multiple_of(h * 64, 64), 64)
            self.DS[rows] = (self.ACC[rows] * self.SL[rows]).astype(jnp.bfloat16)
            return 0

        lax.fori_loop(0, TOKENS // 64, one, 0)

    def gradient(self, level, i):
        q = self.pair(i)
        left = self.T2[level]
        right = (self.DS, self.TB)[level]

        def one(h, _):
            cols = pl.ds(pl.multiple_of(h * 256, 256), 256)
            g = contract_first(left[q, :, cols], right[...]) * (1.0 / TOKENS**0.5)
            self.S[level, q, pl.ds(h * 2, 2)] = g.astype(jnp.bfloat16).reshape(2, 2, NC, PIECE, COLS)
            return 0

        lax.fori_loop(0, CHUNK // 256, one, 0)

    def send_gradient(self, level, i):
        q = self.pair(i)
        for k, (dy, dc) in enumerate(PEERS):
            yy = lax.rem(self.y + dy, NY)
            cc = lax.rem(self.c + dc, NC)
            self.send(
                self.S.at[level, q, yy, :, cc],
                self.R.at[level, k, pl.ds(q * 2, 2)],
                self.yssem.at[level],
                self.yrsem.at[level, i],
                self.dev(dy=dy, dc=dc),
            )

    def wait_gradient(self, level, i):
        q = self.pair(i)
        self.wait(self.R.at[level, :, pl.ds(q * 2, 2)], self.yrsem.at[level, i])

    def passed(self, level, d, use):
        t = lax.rem(self.z + (d + NZ), NZ)
        q = lax.div(t, 2)
        low = lax.rem(t, 2)
        ids = [self.ch[self.path_of() * 2 + level]]
        ids += [self.ch[self.path_of(dy=-dy, dc=-dc) * 2 + level] for dy, dc in PEERS]
        weight = [[jnp.where(i == m, 1.0, 0.0).astype(jnp.float32) for m in range(GRID)] for i in ids]

        def one(b, _):
            cols = pl.ds(pl.multiple_of(b * 128, 128), 128)
            parts = [self.S[level, q, self.y, low, self.c, :, cols].astype(jnp.float32)]
            parts += [self.R[level, k, t, :, cols].astype(jnp.float32) for k in range(NP)]
            for m in range(GRID):
                total = parts[0] * weight[0][m]
                for s in range(1, NP + 1):
                    total = total + parts[s] * weight[s][m]
                use(m, cols, total)
            return 0

        lax.fori_loop(0, COLS // 128, one, 0)

    def hop(self, level, d):
        slot = HOPS.index(d)
        up = d > 0
        came = self.UP if up else self.DOWN
        if d == 4:

            def use(m, cols, total):
                self.SB[level, slot, m, :, cols] = total.astype(jnp.bfloat16)

        else:
            k = abs(d)
            self.wait(self.arriving(level, up, k), (self.usem if up else self.dsem).at[level, k])

            def use(m, cols, total):
                if k < 3 or (m < GRID // 2) == up:
                    total = total + came[level, k, m, :, cols].astype(jnp.float32)
                self.SB[level, slot, m, :, cols] = total.astype(jnp.bfloat16)

        self.passed(level, d, use)
        half = GRID // 2
        if d == 4:
            lo, hi = pl.ds(0, half), pl.ds(half, half)
            self.send(self.SB.at[level, slot, lo], self.UP.at[level, 3, lo], self.zssem.at[level], self.usem.at[level, 3], self.dev(dz=1))
            self.send(self.SB.at[level, slot, hi], self.DOWN.at[level, 3, hi], self.zssem.at[level], self.dsem.at[level, 3], self.dev(dz=-1))
        elif up:
            self.send(self.SB.at[level, slot], self.UP.at[level, d - 1], self.zssem.at[level], self.usem.at[level, d - 1], self.dev(dz=1))
        else:
            self.send(self.SB.at[level, slot], self.DOWN.at[level, -d - 1], self.zssem.at[level], self.dsem.at[level, -d - 1], self.dev(dz=-1))

    def arriving(self, level, up, k):
        half = GRID // 2
        buf = self.UP if up else self.DOWN
        if k == 3:
            return buf.at[level, 3, pl.ds(0 if up else half, half)]
        return buf.at[level, k]

    def counts(self):
        for level in range(2):
            ids = self.chv[:, level : level + 1]
            for m in range(GRID):
                n = jnp.sum(jnp.where(ids == m, 1.0, 0.0), axis=0, keepdims=True)
                self.INV[level, m] = jnp.broadcast_to(1.0 / jnp.maximum(n, 1.0), (8, 128))

    def own(self, level):
        if level == 1:
            self.wait(self.MOM, self.msem.at[0])
        self.wait(self.UP.at[level, 0], self.usem.at[level, 0])
        self.wait(self.DOWN.at[level, 0], self.dsem.at[level, 0])

        def use(m, cols, total):
            total = total + self.UP[level, 0, m, :, cols].astype(jnp.float32)
            total = total + self.DOWN[level, 0, m, :, cols].astype(jnp.float32)
            avg = total * self.INV[level, m, :1]
            mom = MU * self.MOM[level, m, :, cols] + avg
            self.NM[level, m, :, cols] = mom
            self.U[level][0][m, :, cols] = (MU * mom + avg).astype(jnp.bfloat16)

        self.passed(level, 0, use)
        pltpu.make_async_copy(self.NM.at[level], self.nm_hbm.at[level], self.msem.at[1 + level]).start()
        self.spread(level, 0)

    def spread(self, level, d):
        half = GRID // 2
        src = self.U[level][d % NZ]
        if d <= 0:
            to = (d - 1) % NZ
            rows = pl.ds(0, half) if d == -3 else pl.ds(0, GRID)
            self.send(src.at[rows], self.U[level][to].at[rows], self.gssem.at[level], self.gusem.at[level, 1 - d], self.dev(dz=1))
        if d >= 0:
            to = (d + 1) % NZ
            rows = pl.ds(half, half) if d == 3 else pl.ds(0, GRID)
            self.send(src.at[rows], self.U[level][to].at[rows], self.gssem.at[level], self.gdsem.at[level, d + 1], self.dev(dz=-1))

    def wait_spread(self, level, d):
        half = GRID // 2
        buf = self.U[level][d % NZ]
        if d == 4:
            self.wait(buf.at[pl.ds(0, half)], self.gusem.at[level, 4])
            self.wait(buf.at[pl.ds(half, half)], self.gdsem.at[level, 4])
        elif d < 0:
            self.wait(buf, self.gusem.at[level, -d])
        else:
            self.wait(buf, self.gdsem.at[level, d])

    def give(self, level, d):
        t = lax.rem(self.z + (d + NZ), NZ)
        rows = pl.ds(pl.multiple_of((self.y * NZ + t) * (NC * PIECE) + self.c * PIECE, PIECE), PIECE)
        buf = self.U[level][d % NZ]
        dst = self.f_hbm[level].at[rows]
        for k, (dy, dc) in enumerate(PEERS):
            m = self.ch[self.path_of(dy=dy, dc=dc) * 2 + level]
            self.SEL[level, d % NZ, k] = buf[m]
            self.send(self.SEL.at[level, d % NZ, k], dst, self.fssem.at[level], self.frsem.at[level], self.dev(dy=dy, dc=dc))
        m = self.ch[self.path_of() * 2 + level]
        self.SEL[level, d % NZ, NP] = buf[m]
        pltpu.make_async_copy(self.SEL.at[level, d % NZ, NP], dst, self.flsem.at[level]).start()

    def finish(self):
        for level in range(2):
            self.wait(self.f_hbm[level].at[pl.ds(0, D // 8 * 7)], self.frsem.at[level])
            self.wait(self.f_hbm[level].at[pl.ds(0, D // 8)], self.flsem.at[level])
            self.wait(self.SEL.at[level, :, pl.ds(0, NP)], self.fssem.at[level])
            self.wait(self.SB.at[level], self.zssem.at[level])
            self.wait(self.SB.at[level], self.gssem.at[level])
            self.wait(self.R.at[level], self.yssem.at[level])
            self.wait(self.T2[level].at[pl.ds(0, 3)], self.tssem.at[level])
            self.wait(self.NM.at[level], self.msem.at[1 + level])

    def run(self):
        self.load_local()
        self.counts()
        self.barrier()
        for a in (0, 1):
            for i in range(NPAIR):
                self.send_tokens(a, i)
        for i in range(NPAIR):
            self.wait_tokens(0, i)
            self.product(0, i)
        self.activate()
        for i in range(NPAIR):
            self.wait_tokens(1, i)
            self.gradient(1, i)
            self.send_gradient(1, i)
            self.product(1, i)
            if i == 1:
                self.wait_gradient(1, 0)
                self.hop(1, 4)
            if i == 2:
                self.wait_gradient(1, 1)
                self.hop(1, 3)
                self.hop(1, 2)
        self.slope()
        for i in range(NPAIR):
            self.gradient(0, i)
            self.send_gradient(0, i)
        self.wait_gradient(1, 2)
        self.hop(1, -3)
        self.hop(1, -2)
        self.wait_gradient(1, 3)
        self.hop(1, 1)
        self.hop(1, -1)
        self.wait_gradient(0, 0)
        self.hop(0, 4)
        self.own(1)
        self.wait_gradient(0, 1)
        self.hop(0, 3)
        self.hop(0, 2)
        self.give(1, 0)

        def step(level, k):
            for d in (-k, k) if k < 4 else (4,):
                self.wait_spread(level, d)
                if k < 4:
                    self.spread(level, d)
            for d in (-k, k) if k < 4 else (4,):
                self.give(level, d)

        step(1, 1)
        self.wait_gradient(0, 2)
        self.hop(0, -3)
        self.hop(0, -2)
        step(1, 2)
        self.wait_gradient(0, 3)
        self.hop(0, 1)
        self.hop(0, -1)
        step(1, 3)
        self.own(0)
        self.give(0, 0)
        step(1, 4)
        for k in (1, 2, 3, 4):
            step(0, k)
        self.finish()


SCRATCH = dict(
    X=pltpu.VMEM((NPAIR, TOKENS, CHUNK), jnp.bfloat16),
    C=pltpu.VMEM((NPAIR, TOKENS, CHUNK), jnp.bfloat16),
    W1=pltpu.VMEM((NPAIR, CHUNK, COLS), jnp.bfloat16),
    W2=pltpu.VMEM((NPAIR, CHUNK, COLS), jnp.bfloat16),
    ACC=pltpu.VMEM((TOKENS, COLS), jnp.float32),
    SL=pltpu.VMEM((TOKENS, COLS), jnp.float32),
    TB=pltpu.VMEM((TOKENS, COLS), jnp.bfloat16),
    DS=pltpu.VMEM((TOKENS, COLS), jnp.bfloat16),
    S=pltpu.VMEM((2, NPAIR, NY, 2, NC, PIECE, COLS), jnp.bfloat16),
    R=pltpu.VMEM((2, NP, NZ, PIECE, COLS), jnp.bfloat16),
    SB=pltpu.VMEM((2, len(HOPS), GRID, PIECE, COLS), jnp.bfloat16),
    UP=pltpu.VMEM((2, 4, GRID, PIECE, COLS), jnp.bfloat16),
    DOWN=pltpu.VMEM((2, 4, GRID, PIECE, COLS), jnp.bfloat16),
    MOM=pltpu.VMEM((2, GRID, PIECE, COLS), jnp.float32),
    NM=pltpu.VMEM((2, GRID, PIECE, COLS), jnp.float32),
    INV=pltpu.VMEM((2, GRID, 8, 128), jnp.float32),
    SEL=pltpu.VMEM((2, NZ, NP + 1, PIECE, COLS), jnp.bfloat16),
    lsem=pltpu.SemaphoreType.DMA((2, NPAIR)),
    tssem=pltpu.SemaphoreType.DMA((2,)),
    trsem=pltpu.SemaphoreType.DMA((2, NPAIR)),
    yssem=pltpu.SemaphoreType.DMA((2,)),
    yrsem=pltpu.SemaphoreType.DMA((2, NPAIR)),
    zssem=pltpu.SemaphoreType.DMA((2,)),
    usem=pltpu.SemaphoreType.DMA((2, 4)),
    dsem=pltpu.SemaphoreType.DMA((2, 4)),
    gssem=pltpu.SemaphoreType.DMA((2,)),
    gusem=pltpu.SemaphoreType.DMA((2, 5)),
    gdsem=pltpu.SemaphoreType.DMA((2, 5)),
    fssem=pltpu.SemaphoreType.DMA((2,)),
    frsem=pltpu.SemaphoreType.DMA((2,)),
    flsem=pltpu.SemaphoreType.DMA((2,)),
    msem=pltpu.SemaphoreType.DMA((3,)),
)
UPDATES = [pltpu.VMEM((GRID, PIECE, COLS), jnp.bfloat16)] * (2 * NZ)


def kernel(*refs):
    ins, outs, rest = refs[:7], refs[7:10], refs[10:]
    named = dict(zip(SCRATCH, rest))
    body = Body(ins, outs, named)
    updates = rest[len(SCRATCH) :]
    body.U = [updates[:NZ], updates[NZ:]]
    body.T2 = [body.X, body.C]
    body.run()


def sync(acts, cotan, first, second, choose, momentum):
    hbm = pl.BlockSpec(memory_space=pl.ANY)
    return pl.pallas_call(
        kernel,
        out_shape=(
            jax.ShapeDtypeStruct((D, COLS), jnp.bfloat16),
            jax.ShapeDtypeStruct((D, COLS), jnp.bfloat16),
            jax.ShapeDtypeStruct(momentum.shape, jnp.float32),
        ),
        in_specs=[hbm] * 4
        + [pl.BlockSpec(memory_space=pltpu.SMEM), pl.BlockSpec(memory_space=pltpu.VMEM), hbm],
        out_specs=[hbm] * 3,
        scratch_shapes=list(SCRATCH.values()) + UPDATES,
        compiler_params=pltpu.CompilerParams(
            collective_id=0, has_side_effects=True, vmem_limit_bytes=58 * 2**20
        ),
        cost_estimate=pl.CostEstimate(flops=8 * 10**9, bytes_accessed=2 * 10**7, transcendentals=0),
    )(acts, cotan, first, second, choose.reshape(-1), choose, momentum)


def on_device(acts, cotan, w_in, w_out_t, choose, momentum):
    first, second = w_in[0], w_out_t[0]
    update_in, update_out, new_momentum = sync(acts, cotan, first, second, choose, momentum)

    def apply(weight, update):
        return (weight.astype(jnp.float32) - OUTER_LR * update.astype(jnp.float32)).astype(jnp.bfloat16)

    return (apply(first, update_in)[None], apply(second, update_out)[None], new_momentum)


def solution(mesh):
    return jax.shard_map(
        on_device,
        mesh=mesh,
        in_specs=(
            P(("path", "inner"), None),
            P(("path", "inner"), None),
            P("path", None, "inner"),
            P("path", None, "inner"),
            P(),
            P(None, None, "path", "inner"),
        ),
        out_specs=(
            P("path", None, "inner"),
            P("path", None, "inner"),
            P(None, None, "path", "inner"),
        ),
        check_vma=False,
    )
```

```python
import functools

import jax
import jax.numpy as jnp
from jax import lax
from jax.experimental import pallas as pl
from jax.experimental.pallas import tpu as pltpu
from jax.sharding import PartitionSpec as P

MU = 0.9
OUTER_LR = 0.7
MESH = pl.DeviceIdType.MESH

NX, NY, NZ, NC = 4, 4, 8, 2
GRID = 8
TOK = 256
TOKENS = TOK * NX
D = 2048
COLS = D // NX
PIECE = D // (NY * NZ * NC)
NPAIR = NZ // 2
PAIR = 2 * NC * PIECE
CHUNK = NY * PAIR
PEERS = [(2, 0), (2, 1), (1, 0), (1, 1), (3, 0), (3, 1), (0, 1)]
NP = len(PEERS)
ORDER = [2, 1, 3, 0]
AHEAD = 2
SCHEDULE = [
    ("forward_tokens", 0),
    ("forward_tokens", 1),
    ("product", 0, 0),
    ("forward_tokens", 2),
    ("product", 0, 1),
    ("forward_tokens", 3),
    ("product", 0, 2),
    ("forward_tokens", 4),
    ("product", 0, 3),
    ("activate",),
    ("forward_tokens", 5),
    ("gradient", 1, 0),
    ("product", 1, 0),
    ("forward_tokens", 6),
    ("hop", 1, 4, 0),
    ("hop", 1, 4, 1),
    ("gradient", 1, 1),
    ("product", 1, 1),
    ("forward_tokens", 7),
    ("gradient", 1, 2),
    ("hop", 1, 3, 0),
    ("hop", 1, 3, 1),
    ("product", 1, 2),
    ("gradient", 1, 3),
    ("product", 1, 3),
    ("slope",),
    ("gradient", 0, 0),
    ("gradient", 0, 1),
    ("hop", 1, -3, 0),
    ("hop", 1, -3, 1),
    ("gradient", 0, 2),
    ("gradient", 0, 3),
    ("hop", 1, 2, 0),
    ("hop", 1, 2, 1),
    ("hop", 1, -2, 0),
    ("hop", 1, -2, 1),
    ("hop", 1, 1, 0),
    ("hop", 1, -1, 0),
    ("hop", 0, 4, 0),
    ("hop", 0, 4, 1),
    ("hop", 1, 1, 1),
    ("hop", 1, -1, 1),
    ("own", 1, 0),
    ("hop", 0, 3, 0),
    ("hop", 0, 3, 1),
    ("own", 1, 1),
    ("hop", 0, -3, 0),
    ("hop", 0, -3, 1),
    ("give", 1, 0),
    ("spread", 1, -1, 0),
    ("spread", 1, 1, 0),
    ("hop", 0, 2, 0),
    ("spread", 1, 1, 1),
    ("give", 1, 1),
    ("hop", 0, 2, 1),
    ("hop", 0, -2, 0),
    ("spread", 1, -1, 1),
    ("give", 1, -1),
    ("hop", 0, -2, 1),
    ("spread", 1, -2, 0),
    ("spread", 1, 2, 0),
    ("hop", 0, 1, 0),
    ("spread", 1, 2, 1),
    ("give", 1, 2),
    ("hop", 0, 1, 1),
    ("hop", 0, -1, 0),
    ("spread", 1, -2, 1),
    ("give", 1, -2),
    ("hop", 0, -1, 1),
    ("spread", 1, -3, 0),
    ("spread", 1, 3, 0),
    ("spread", 1, 3, 1),
    ("give", 1, 3),
    ("own", 0, 0),
    ("spread", 1, -3, 1),
    ("give", 1, -3),
    ("own", 0, 1),
    ("give", 0, 0),
    ("spread", 0, -1, 0),
    ("give", 1, 4),
    ("spread", 0, 1, 0),
    ("spread", 0, -1, 1),
    ("give", 0, -1),
    ("spread", 0, 1, 1),
    ("give", 0, 1),
    ("spread", 0, -2, 0),
    ("spread", 0, 2, 0),
    ("spread", 0, -2, 1),
    ("give", 0, -2),
    ("spread", 0, 2, 1),
    ("give", 0, 2),
    ("spread", 0, -3, 0),
    ("spread", 0, 3, 0),
    ("spread", 0, -3, 1),
    ("give", 0, -3),
    ("spread", 0, 3, 1),
    ("give", 0, 3),
    ("give", 0, 4),
]
HOPS = [4, 3, 2, 1, -3, -2, -1]
READY = {4: 0, 3: 1, 2: 1, -3: 2, -2: 2, 1: 3, -1: 3, 0: 3}
PARTS = 2
WIDTH = COLS // PARTS


def contract_first(left, right):
    return lax.dot_general(
        left, right, (((0,), (0,)), ((), ())), preferred_element_type=jnp.float32
    )


class Body:
    def __init__(self, ins, outs, scratch):
        self.x_hbm, self.c_hbm, self.w1_hbm, self.w2_hbm, self.ch, self.chv, self.mom_hbm = ins
        self.f_hbm = outs[:2]
        self.nm_hbm = outs[2]
        for name, ref in scratch.items():
            setattr(self, name, ref)
        path = lax.axis_index("path")
        self.x = lax.axis_index("inner")
        self.y = lax.div(path, NZ * NC)
        self.z = lax.rem(lax.div(path, NC), NZ)
        self.c = lax.rem(path, NC)
        self.zp = lax.div(self.z, 2)

    def path_of(self, dy=0, dz=0, dc=0):
        y = lax.rem(self.y + (dy + NY), NY)
        z = lax.rem(self.z + (dz + NZ), NZ)
        c = lax.rem(self.c + (dc + NC), NC)
        return (y * NZ + z) * NC + c

    def dev(self, dy=0, dz=0, dc=0, dx=0):
        return (self.path_of(dy, dz, dc), lax.rem(self.x + (dx + NX), NX))

    def send(self, src, dst, ssem, rsem, dev):
        pltpu.make_async_remote_copy(
            src_ref=src, dst_ref=dst, send_sem=ssem, recv_sem=rsem, device_id=dev, device_id_type=MESH
        ).start()

    def wait(self, ref, sem):
        pltpu.make_async_copy(ref, ref, sem).wait()

    def barrier(self):
        bar = pltpu.get_barrier_semaphore()
        partners = [self.dev(dx=1), self.dev(dx=-1)]
        partners += [self.dev(dy=dy, dc=dc) for dy, dc in PEERS]
        partners += [self.dev(dz=1), self.dev(dz=-1)]
        for partner in partners:
            pl.semaphore_signal(bar, inc=1, device_id=partner, device_id_type=MESH)
        pl.semaphore_wait(bar, len(partners))

    def pair(self, i):
        return lax.rem(self.zp + ORDER[i], NPAIR)

    def load_local(self):
        for a, (hbm, whbm, wbuf) in enumerate(
            ((self.x_hbm, self.w1_hbm, self.W1), (self.c_hbm, self.w2_hbm, self.W2))
        ):
            for i in range(NPAIR):
                q = self.pair(i)

                def tokens(yy, _, a=a, i=i, q=q, hbm=hbm):
                    cols = pl.multiple_of(yy * (NPAIR * PAIR) + q * PAIR, PAIR)
                    pltpu.make_async_copy(
                        hbm.at[:, pl.ds(cols, PAIR)], self.T2[a].at[q, yy, self.x], self.lsem.at[a, i]
                    ).start()
                    return 0

                lax.fori_loop(0, NY, tokens, 0)
            for i in range(NPAIR):
                q = self.pair(i)

                def weights(yy, _, a=a, i=i, q=q, whbm=whbm, wbuf=wbuf):
                    rows = pl.multiple_of(yy * (NPAIR * PAIR) + q * PAIR, PAIR)
                    place = pl.multiple_of(yy * PAIR, PAIR)
                    pltpu.make_async_copy(
                        whbm.at[pl.ds(rows, PAIR)], wbuf.at[q, pl.ds(place, PAIR)], self.wsem.at[a, i]
                    ).start()
                    return 0

                lax.fori_loop(0, NY, weights, 0)
        pltpu.make_async_copy(self.mom_hbm, self.MOM, self.msem.at[0]).start()

    def send_tokens(self, n):
        a, i = divmod(n, NPAIR)
        own = self.T2[a].at[self.pair(i), :, self.x]
        self.wait(own, self.lsem.at[a, i])
        for k, dx in enumerate((1, -1)):
            self.send(own, own, self.tssem.at[a], self.trsem.at[a, i, k], self.dev(dx=dx))

    def forward_tokens(self, n):
        a, i = divmod(n, NPAIR)
        q = self.pair(i)
        for k, dx in enumerate((1, -1)):
            src = lax.rem(self.x + (NX - dx), NX)
            self.wait(self.T2[a].at[q, :, src], self.trsem.at[a, i, k])
            half = self.T2[a].at[q, pl.ds(k * (NY // 2), NY // 2), src]
            self.send(half, half, self.tssem.at[a], self.trsem.at[a, i, 2], self.dev(dx=dx))
        if n + AHEAD < 2 * NPAIR:
            self.send_tokens(n + AHEAD)

    def wait_tokens(self, n):
        if n in self.came:
            return
        self.came.add(n)
        a, i = divmod(n, NPAIR)
        q = self.pair(i)
        self.wait((self.W1, self.W2)[a].at[q], self.wsem.at[a, i])
        self.wait(self.T2[a].at[q, :, lax.rem(self.x + 2, NX)], self.trsem.at[a, i, 2])

    def product(self, a, i):
        self.wait_tokens(a * NPAIR + i)
        q = self.pair(i)
        wbuf = (self.W1, self.W2)[a]

        def one(h, _):
            rows = pl.ds(pl.multiple_of(h * 512, 512), 512)
            left = jnp.concatenate(
                [self.T2[a][q, yy, pl.ds(h * 2, 2)].reshape(512, PAIR) for yy in range(NY)], axis=1
            )
            part = jnp.dot(left, wbuf[q], preferred_element_type=jnp.float32)
            if i == 0:
                self.ACC[rows] = part
            else:
                self.ACC[rows] = self.ACC[rows] + part
            return 0

        lax.fori_loop(0, TOKENS // 512, one, 0)

    def activate(self):
        def one(h, _):
            rows = pl.ds(pl.multiple_of(h * 64, 64), 64)
            t = jnp.tanh(self.ACC[rows])
            self.TB[rows] = t.astype(jnp.bfloat16)
            self.SL[rows] = 1.0 - t * t
            return 0

        lax.fori_loop(0, TOKENS // 64, one, 0)

    def slope(self):
        def one(h, _):
            rows = pl.ds(pl.multiple_of(h * 64, 64), 64)
            self.DS[rows] = (self.ACC[rows] * self.SL[rows]).astype(jnp.bfloat16)
            return 0

        lax.fori_loop(0, TOKENS // 64, one, 0)

    def gradient(self, level, i):
        if level == 1:
            self.wait_tokens(NPAIR + i)
        q = self.pair(i)
        left = self.T2[level]
        right = (self.DS, self.TB)[level]

        def one(h, _):
            cols = jnp.concatenate([left[q, h * 2 + e].reshape(TOKENS, PAIR) for e in range(2)], axis=1)
            g = contract_first(cols, right[...]) * (1.0 / TOKENS**0.5)
            self.S[level, q, pl.ds(h * 2, 2)] = g.astype(jnp.bfloat16).reshape(2, 2, NC, PIECE, COLS)
            return 0

        lax.fori_loop(0, CHUNK // 256, one, 0)
        for k, (dy, dc) in enumerate(PEERS):
            yy = lax.rem(self.y + dy, NY)
            cc = lax.rem(self.c + dc, NC)
            self.send(
                self.S.at[level, q, yy, :, cc],
                self.R.at[level, k, pl.ds(q * 2, 2)],
                self.yssem.at[level],
                self.yrsem.at[level, i],
                self.dev(dy=dy, dc=dc),
            )

    def wait_gradient(self, level, i):
        if (level, i) in self.came:
            return
        self.came.add((level, i))
        q = self.pair(i)
        self.wait(self.R.at[level, :, pl.ds(q * 2, 2)], self.yrsem.at[level, i])

    def passed(self, level, d, h, use):
        t = lax.rem(self.z + (d + NZ), NZ)
        q = lax.div(t, 2)
        low = lax.rem(t, 2)
        ids = [self.ch[self.path_of() * 2 + level]]
        ids += [self.ch[self.path_of(dy=-dy, dc=-dc) * 2 + level] for dy, dc in PEERS]
        weight = [[jnp.where(i == m, 1.0, 0.0).astype(jnp.float32) for m in range(GRID)] for i in ids]

        def one(b, _):
            cols = pl.ds(pl.multiple_of(h * WIDTH + b * 128, 128), 128)
            parts = [self.S[level, q, self.y, low, self.c, :, cols].astype(jnp.float32)]
            parts += [self.R[level, k, t, :, cols].astype(jnp.float32) for k in range(NP)]
            for m in range(GRID):
                total = parts[0] * weight[0][m]
                for s in range(1, NP + 1):
                    total = total + parts[s] * weight[s][m]
                use(m, cols, pl.ds(pl.multiple_of(b * 128, 128), 128), total)
            return 0

        lax.fori_loop(0, WIDTH // 128, one, 0)

    def hop(self, level, d, h):
        self.wait_gradient(level, READY[d])
        slot = HOPS.index(d)
        up = d > 0
        k = abs(d)
        came = self.UP if up else self.DOWN
        if k < 4:
            self.wait(self.arriving(level, up, k, h), (self.usem if up else self.dsem).at[level, k, h])

        def use(m, cols, place, total):
            if k < 3 or k == 3 and (m < GRID // 2) == up:
                total = total + came[level, k, h, m, :, place].astype(jnp.float32)
            self.SB[level, slot, h, m, :, place] = total.astype(jnp.bfloat16)

        self.passed(level, d, h, use)
        sum_ref, ssem = self.SB.at[level, slot, h], self.zssem.at[level]
        if up:
            rows = pl.ds(0, GRID // 2 if k == 4 else GRID)
            self.send(sum_ref.at[rows], self.UP.at[level, k - 1, h, rows], ssem, self.usem.at[level, k - 1, h], self.dev(dz=1))
        if not up or k == 4:
            rows = pl.ds(GRID // 2, GRID // 2) if k == 4 else pl.ds(0, GRID)
            self.send(sum_ref.at[rows], self.DOWN.at[level, k - 1, h, rows], ssem, self.dsem.at[level, k - 1, h], self.dev(dz=-1))

    def arriving(self, level, up, k, h):
        half = GRID // 2
        buf = self.UP if up else self.DOWN
        if k == 3:
            return buf.at[level, 3, h, pl.ds(0 if up else half, half)]
        return buf.at[level, k, h]

    def counts(self):
        for level in range(2):
            ids = self.chv[:, level : level + 1]
            for m in range(GRID):
                n = jnp.sum(jnp.where(ids == m, 1.0, 0.0), axis=0, keepdims=True)
                self.INV[level, m] = jnp.broadcast_to(1.0 / jnp.maximum(n, 1.0), (8, 128))

    def own(self, level, h):
        self.wait_gradient(level, READY[0])
        if "momentum" not in self.came:
            self.came.add("momentum")
            self.wait(self.MOM, self.msem.at[0])
        self.wait(self.UP.at[level, 0, h], self.usem.at[level, 0, h])
        self.wait(self.DOWN.at[level, 0, h], self.dsem.at[level, 0, h])

        def use(m, cols, place, total):
            total = total + self.UP[level, 0, h, m, :, place].astype(jnp.float32)
            total = total + self.DOWN[level, 0, h, m, :, place].astype(jnp.float32)
            avg = total * self.INV[level, m, :1]
            mom = MU * self.MOM[level, m, :, cols] + avg
            self.NM[level, m, :, cols] = mom
            self.U[level][0][h, m, :, place] = (MU * mom + avg).astype(jnp.bfloat16)

        self.passed(level, 0, h, use)
        self.pass_on(level, 0, h)
        if h == PARTS - 1:
            pltpu.make_async_copy(self.NM.at[level], self.nm_hbm.at[level], self.msem.at[1 + level]).start()

    def pass_on(self, level, d, h):
        half = GRID // 2
        src = self.U[level][d % NZ].at[h]
        ssem = self.gssem.at[level]
        if d <= 0:
            to = self.U[level][(d - 1) % NZ].at[h]
            rows = pl.ds(0, half if d == -3 else GRID)
            self.send(src.at[rows], to.at[rows], ssem, self.gusem.at[level, 1 - d, h], self.dev(dz=1))
        if d >= 0:
            to = self.U[level][(d + 1) % NZ].at[h]
            rows = pl.ds(half, half) if d == 3 else pl.ds(0, GRID)
            self.send(src.at[rows], to.at[rows], ssem, self.gdsem.at[level, d + 1, h], self.dev(dz=-1))

    def spread(self, level, d, h):
        sem = self.gusem.at[level, -d, h] if d < 0 else self.gdsem.at[level, d, h]
        self.wait(self.U[level][d % NZ].at[h], sem)
        self.pass_on(level, d, h)

    def give(self, level, d):
        t = lax.rem(self.z + (d + NZ), NZ)
        rows = pl.ds(pl.multiple_of((self.y * NZ + t) * (NC * PIECE) + self.c * PIECE, PIECE), PIECE)
        buf = self.U[level][d % NZ]
        if d == 4:
            half = GRID // 2
            for h in range(PARTS):
                self.wait(buf.at[h, pl.ds(0, half)], self.gusem.at[level, 4, h])
                self.wait(buf.at[h, pl.ds(half, half)], self.gdsem.at[level, 4, h])
        dst = self.f_hbm[level].at[rows]
        for k, (dy, dc) in enumerate(PEERS + [(0, 0)]):
            m = self.ch[self.path_of(dy=dy, dc=dc) * 2 + level]
            src = self.SEL.at[level, d % NZ, k]
            for h in range(PARTS):
                src[:, h * WIDTH : (h + 1) * WIDTH] = buf[h, m]
            if k < NP:
                self.send(src, dst, self.fssem.at[level], self.frsem.at[level], self.dev(dy=dy, dc=dc))
            else:
                pltpu.make_async_copy(src, dst, self.flsem.at[level]).start()

    def finish(self):
        for level in range(2):
            self.wait(self.f_hbm[level].at[pl.ds(0, D // 8 * 7)], self.frsem.at[level])
            self.wait(self.f_hbm[level].at[pl.ds(0, D // 8)], self.flsem.at[level])
            self.wait(self.SEL.at[level, :, pl.ds(0, NP)], self.fssem.at[level])
            self.wait(self.SB.at[level], self.zssem.at[level])
            self.wait(self.SB.at[level], self.gssem.at[level])
            self.wait(self.R.at[level], self.yssem.at[level])
            self.wait(self.T2[level].at[pl.ds(0, 3)], self.tssem.at[level])
            self.wait(self.NM.at[level], self.msem.at[1 + level])

    def run(self):
        self.came = set()
        self.load_local()
        self.counts()
        self.barrier()
        for n in range(AHEAD):
            self.send_tokens(n)
        for step, *args in SCHEDULE:
            getattr(self, step)(*args)
        self.finish()


SCRATCH = dict(
    X=pltpu.VMEM((NPAIR, NY, NX, TOK, PAIR), jnp.bfloat16),
    C=pltpu.VMEM((NPAIR, NY, NX, TOK, PAIR), jnp.bfloat16),
    W1=pltpu.VMEM((NPAIR, CHUNK, COLS), jnp.bfloat16),
    W2=pltpu.VMEM((NPAIR, CHUNK, COLS), jnp.bfloat16),
    ACC=pltpu.VMEM((TOKENS, COLS), jnp.float32),
    SL=pltpu.VMEM((TOKENS, COLS), jnp.float32),
    TB=pltpu.VMEM((TOKENS, COLS), jnp.bfloat16),
    DS=pltpu.VMEM((TOKENS, COLS), jnp.bfloat16),
    S=pltpu.VMEM((2, NPAIR, NY, 2, NC, PIECE, COLS), jnp.bfloat16),
    R=pltpu.VMEM((2, NP, NZ, PIECE, COLS), jnp.bfloat16),
    SB=pltpu.VMEM((2, len(HOPS), PARTS, GRID, PIECE, WIDTH), jnp.bfloat16),
    UP=pltpu.VMEM((2, 4, PARTS, GRID, PIECE, WIDTH), jnp.bfloat16),
    DOWN=pltpu.VMEM((2, 4, PARTS, GRID, PIECE, WIDTH), jnp.bfloat16),
    MOM=pltpu.VMEM((2, GRID, PIECE, COLS), jnp.float32),
    NM=pltpu.VMEM((2, GRID, PIECE, COLS), jnp.float32),
    INV=pltpu.VMEM((2, GRID, 8, 128), jnp.float32),
    SEL=pltpu.VMEM((2, NZ, NP + 1, PIECE, COLS), jnp.bfloat16),
    lsem=pltpu.SemaphoreType.DMA((2, NPAIR)),
    wsem=pltpu.SemaphoreType.DMA((2, NPAIR)),
    tssem=pltpu.SemaphoreType.DMA((2,)),
    trsem=pltpu.SemaphoreType.DMA((2, NPAIR, 3)),
    yssem=pltpu.SemaphoreType.DMA((2,)),
    yrsem=pltpu.SemaphoreType.DMA((2, NPAIR)),
    zssem=pltpu.SemaphoreType.DMA((2,)),
    usem=pltpu.SemaphoreType.DMA((2, 4, PARTS)),
    dsem=pltpu.SemaphoreType.DMA((2, 4, PARTS)),
    gssem=pltpu.SemaphoreType.DMA((2,)),
    gusem=pltpu.SemaphoreType.DMA((2, 5, PARTS)),
    gdsem=pltpu.SemaphoreType.DMA((2, 5, PARTS)),
    fssem=pltpu.SemaphoreType.DMA((2,)),
    frsem=pltpu.SemaphoreType.DMA((2,)),
    flsem=pltpu.SemaphoreType.DMA((2,)),
    msem=pltpu.SemaphoreType.DMA((3,)),
)
UPDATES = [pltpu.VMEM((PARTS, GRID, PIECE, WIDTH), jnp.bfloat16)] * (2 * NZ)


def kernel(*refs):
    ins, outs, rest = refs[:7], refs[7:10], refs[10:]
    named = dict(zip(SCRATCH, rest))
    body = Body(ins, outs, named)
    updates = rest[len(SCRATCH) :]
    body.U = [updates[:NZ], updates[NZ:]]
    body.T2 = [body.X, body.C]
    body.run()


def sync(acts, cotan, first, second, choose, momentum):
    hbm = pl.BlockSpec(memory_space=pl.ANY)
    return pl.pallas_call(
        kernel,
        out_shape=(
            jax.ShapeDtypeStruct((D, COLS), jnp.bfloat16),
            jax.ShapeDtypeStruct((D, COLS), jnp.bfloat16),
            jax.ShapeDtypeStruct(momentum.shape, jnp.float32),
        ),
        in_specs=[hbm] * 4
        + [pl.BlockSpec(memory_space=pltpu.SMEM), pl.BlockSpec(memory_space=pltpu.VMEM), hbm],
        out_specs=[hbm] * 3,
        scratch_shapes=list(SCRATCH.values()) + UPDATES,
        compiler_params=pltpu.CompilerParams(
            collective_id=0, has_side_effects=True, vmem_limit_bytes=58 * 2**20
        ),
        cost_estimate=pl.CostEstimate(flops=8 * 10**9, bytes_accessed=2 * 10**7, transcendentals=0),
    )(acts, cotan, first, second, choose.reshape(-1), choose, momentum)


def on_device(acts, cotan, w_in, w_out_t, choose, momentum):
    first, second = w_in[0], w_out_t[0]
    update_in, update_out, new_momentum = sync(acts, cotan, first, second, choose, momentum)

    def apply(weight, update):
        return (weight.astype(jnp.float32) - OUTER_LR * update.astype(jnp.float32)).astype(jnp.bfloat16)

    return (apply(first, update_in)[None], apply(second, update_out)[None], new_momentum)


def solution(mesh):
    return jax.shard_map(
        on_device,
        mesh=mesh,
        in_specs=(
            P(("path", "inner"), None),
            P(("path", "inner"), None),
            P("path", None, "inner"),
            P("path", None, "inner"),
            P(),
            P(None, None, "path", "inner"),
        ),
        out_specs=(
            P("path", None, "inner"),
            P("path", None, "inner"),
            P(None, None, "path", "inner"),
        ),
        check_vma=False,
    )
```

```python
import functools

import jax
import jax.numpy as jnp
from jax import lax
from jax.experimental import pallas as pl
from jax.experimental.pallas import tpu as pltpu
from jax.sharding import PartitionSpec as P

MU = 0.9
OUTER_LR = 0.7
MESH = pl.DeviceIdType.MESH

NX, NY, NZ, NC = 4, 4, 8, 2
GRID = 8
TOK = 256
TOKENS = TOK * NX
D = 2048
COLS = D // NX
PIECE = D // (NY * NZ * NC)
NPAIR = NZ // 2
PAIR = 2 * NC * PIECE
CHUNK = NY * PAIR
PEERS = [(2, 0), (2, 1), (1, 0), (1, 1), (3, 0), (3, 1), (0, 1)]
NP = len(PEERS)
ORDER = [2, 1, 3, 0]
AHEAD = 2
SCHEDULE = [
    ("forward_tokens", 0),
    ("forward_tokens", 1),
    ("product", 0, 0),
    ("forward_tokens", 2),
    ("product", 0, 1),
    ("forward_tokens", 3),
    ("product", 0, 2),
    ("forward_tokens", 4),
    ("product", 0, 3),
    ("activate",),
    ("forward_tokens", 5),
    ("product", 1, 0),
    ("gradient", 1, 0),
    ("send_gradient", 1, 0, 1),
    ("send_gradient", 1, 0, 0),
    ("forward_tokens", 6),
    ("hop", 1, 4, 1),
    ("gradient", 1, 1),
    ("send_gradient", 1, 1, 1),
    ("product", 1, 1),
    ("send_gradient", 1, 1, 0),
    ("hop", 1, 4, 0),
    ("hop", 1, 3, 1),
    ("forward_tokens", 7),
    ("hop", 1, 3, 0),
    ("gradient", 1, 2),
    ("send_gradient", 1, 2, 0),
    ("product", 1, 2),
    ("send_gradient", 1, 2, 1),
    ("gradient", 1, 3),
    ("send_gradient", 1, 3, 0),
    ("send_gradient", 1, 3, 1),
    ("hop", 1, 2, 1),
    ("hop", 1, -3, 0),
    ("hop", 1, 2, 0),
    ("product", 1, 3),
    ("slope",),
    ("gradient", 0, 1),
    ("hop", 1, -3, 1),
    ("gradient", 0, 0),
    ("send_gradient", 0, 0, 1),
    ("gradient", 0, 2),
    ("hop", 1, -2, 0),
    ("send_gradient", 0, 0, 0),
    ("send_gradient", 0, 2, 0),
    ("send_gradient", 0, 1, 0),
    ("hop", 1, 1, 0),
    ("hop", 1, -2, 1),
    ("send_gradient", 0, 2, 1),
    ("gradient", 0, 3),
    ("send_gradient", 0, 3, 0),
    ("hop", 1, 1, 1),
    ("hop", 1, -1, 0),
    ("hop", 0, 4, 1),
    ("send_gradient", 0, 1, 1),
    ("send_gradient", 0, 3, 1),
    ("hop", 1, -1, 1),
    ("hop", 0, 4, 0),
    ("own", 1, 0),
    ("hop", 0, 3, 0),
    ("own", 1, 1),
    ("give", 1, 0),
    ("spread", 1, -1, 0),
    ("hop", 0, -3, 0),
    ("hop", 0, -3, 1),
    ("hop", 0, 2, 0),
    ("spread", 1, 1, 0),
    ("spread", 1, -1, 1),
    ("give", 1, -1),
    ("hop", 0, 3, 1),
    ("spread", 1, 1, 1),
    ("give", 1, 1),
    ("spread", 1, -2, 0),
    ("hop", 0, -2, 0),
    ("hop", 0, 1, 0),
    ("hop", 0, -2, 1),
    ("spread", 1, -2, 1),
    ("give", 1, -2),
    ("spread", 1, 2, 0),
    ("hop", 0, 2, 1),
    ("spread", 1, 2, 1),
    ("give", 1, 2),
    ("spread", 1, -3, 0),
    ("hop", 0, -1, 0),
    ("hop", 0, -1, 1),
    ("spread", 1, -3, 1),
    ("give", 1, -3),
    ("spread", 1, 3, 0),
    ("hop", 0, 1, 1),
    ("spread", 1, 3, 1),
    ("give", 1, 3),
    ("own", 0, 0),
    ("own", 0, 1),
    ("give", 0, 0),
    ("spread", 0, -1, 0),
    ("give", 1, 4),
    ("spread", 0, -1, 1),
    ("spread", 0, 1, 0),
    ("give", 0, -1),
    ("spread", 0, -2, 0),
    ("spread", 0, 1, 1),
    ("give", 0, 1),
    ("spread", 0, -2, 1),
    ("spread", 0, 2, 0),
    ("give", 0, -2),
    ("spread", 0, -3, 0),
    ("spread", 0, 2, 1),
    ("give", 0, 2),
    ("spread", 0, -3, 1),
    ("spread", 0, 3, 0),
    ("give", 0, -3),
    ("spread", 0, 3, 1),
    ("give", 0, 3),
    ("give", 0, 4),
]
HOPS = [4, 3, 2, 1, -3, -2, -1]
READY = {4: 0, 3: 1, 2: 1, -3: 2, -2: 2, 1: 3, -1: 3, 0: 3}
PARTS = 2
WIDTH = COLS // PARTS


def contract_first(left, right):
    return lax.dot_general(
        left, right, (((0,), (0,)), ((), ())), preferred_element_type=jnp.float32
    )


class Body:
    def __init__(self, ins, outs, scratch):
        self.x_hbm, self.c_hbm, self.w1_hbm, self.w2_hbm, self.ch, self.mom_hbm = ins
        self.f_hbm = outs[:2]
        self.nm_hbm = outs[2]
        for name, ref in scratch.items():
            setattr(self, name, ref)
        path = lax.axis_index("path")
        self.x = lax.axis_index("inner")
        self.y = lax.div(path, NZ * NC)
        self.z = lax.rem(lax.div(path, NC), NZ)
        self.c = lax.rem(path, NC)
        self.zp = lax.div(self.z, 2)

    def path_of(self, dy=0, dz=0, dc=0):
        y = lax.rem(self.y + (dy + NY), NY)
        z = lax.rem(self.z + (dz + NZ), NZ)
        c = lax.rem(self.c + (dc + NC), NC)
        return (y * NZ + z) * NC + c

    def dev(self, dy=0, dz=0, dc=0, dx=0):
        return (self.path_of(dy, dz, dc), lax.rem(self.x + (dx + NX), NX))

    def send(self, src, dst, ssem, rsem, dev):
        pltpu.make_async_remote_copy(
            src_ref=src, dst_ref=dst, send_sem=ssem, recv_sem=rsem, device_id=dev, device_id_type=MESH
        ).start()

    def wait(self, ref, sem):
        pltpu.make_async_copy(ref, ref, sem).wait()

    def barrier(self):
        bar = pltpu.get_barrier_semaphore()
        partners = [self.dev(dx=1), self.dev(dx=-1)]
        partners += [self.dev(dy=dy, dc=dc) for dy, dc in PEERS]
        partners += [self.dev(dz=1), self.dev(dz=-1)]
        for partner in partners:
            pl.semaphore_signal(bar, inc=1, device_id=partner, device_id_type=MESH)
        self.load_local()
        pl.semaphore_wait(bar, len(partners))

    def pair(self, i):
        return lax.rem(self.zp + ORDER[i], NPAIR)

    def load_local(self):
        for a, (hbm, whbm, wbuf) in enumerate(
            ((self.x_hbm, self.w1_hbm, self.W1), (self.c_hbm, self.w2_hbm, self.W2))
        ):
            for i in range(NPAIR):
                q = self.pair(i)

                def tokens(yy, _, a=a, i=i, q=q, hbm=hbm):
                    cols = pl.multiple_of(yy * (NPAIR * PAIR) + q * PAIR, PAIR)
                    pltpu.make_async_copy(
                        hbm.at[:, pl.ds(cols, PAIR)], self.T2[a].at[q, yy, self.x], self.lsem.at[a, i]
                    ).start()
                    return 0

                lax.fori_loop(0, NY, tokens, 0)
            for i in range(NPAIR):
                q = self.pair(i)

                def weights(yy, _, a=a, i=i, q=q, whbm=whbm, wbuf=wbuf):
                    rows = pl.multiple_of(yy * (NPAIR * PAIR) + q * PAIR, PAIR)
                    place = pl.multiple_of(yy * PAIR, PAIR)
                    pltpu.make_async_copy(
                        whbm.at[pl.ds(rows, PAIR)], wbuf.at[q, pl.ds(place, PAIR)], self.wsem.at[a, i]
                    ).start()
                    return 0

                lax.fori_loop(0, NY, weights, 0)
        pltpu.make_async_copy(self.mom_hbm, self.MOM, self.msem.at[0]).start()

    def send_tokens(self, n):
        a, i = divmod(n, NPAIR)
        own = self.T2[a].at[self.pair(i), :, self.x]
        self.wait(own, self.lsem.at[a, i])
        for k, dx in enumerate((1, -1)):
            self.send(own, own, self.tssem.at[a], self.trsem.at[a, i, k], self.dev(dx=dx))

    def forward_tokens(self, n):
        a, i = divmod(n, NPAIR)
        q = self.pair(i)
        for k, dx in enumerate((1, -1)):
            src = lax.rem(self.x + (NX - dx), NX)
            self.wait(self.T2[a].at[q, :, src], self.trsem.at[a, i, k])
            half = self.T2[a].at[q, pl.ds(k * (NY // 2), NY // 2), src]
            self.send(half, half, self.tssem.at[a], self.trsem.at[a, i, 2], self.dev(dx=dx))
        if n + AHEAD < 2 * NPAIR:
            self.send_tokens(n + AHEAD)

    def wait_tokens(self, n):
        if n in self.came:
            return
        self.came.add(n)
        a, i = divmod(n, NPAIR)
        q = self.pair(i)
        self.wait((self.W1, self.W2)[a].at[q], self.wsem.at[a, i])
        self.wait(self.T2[a].at[q, :, lax.rem(self.x + 2, NX)], self.trsem.at[a, i, 2])

    def product(self, a, i):
        self.wait_tokens(a * NPAIR + i)
        q = self.pair(i)
        wbuf = (self.W1, self.W2)[a]

        def one(h, _):
            rows = pl.ds(pl.multiple_of(h * 512, 512), 512)
            left = jnp.concatenate(
                [self.T2[a][q, yy, pl.ds(h * 2, 2)].reshape(512, PAIR) for yy in range(NY)], axis=1
            )
            part = jnp.dot(left, wbuf[q], preferred_element_type=jnp.float32)
            if i == 0:
                self.ACC[rows] = part
            else:
                self.ACC[rows] = self.ACC[rows] + part
            return 0

        lax.fori_loop(0, TOKENS // 512, one, 0)

    def activate(self):
        def one(h, _):
            rows = pl.ds(pl.multiple_of(h * 64, 64), 64)
            t = jnp.tanh(self.ACC[rows])
            self.TB[rows] = t.astype(jnp.bfloat16)
            self.SL[rows] = 1.0 - t * t
            return 0

        lax.fori_loop(0, TOKENS // 64, one, 0)

    def slope(self):
        def one(h, _):
            rows = pl.ds(pl.multiple_of(h * 64, 64), 64)
            self.DS[rows] = (self.ACC[rows] * self.SL[rows]).astype(jnp.bfloat16)
            return 0

        lax.fori_loop(0, TOKENS // 64, one, 0)

    def gradient(self, level, i):
        if level == 1:
            self.wait_tokens(NPAIR + i)
        q = self.pair(i)
        left = self.T2[level]
        right = (self.DS, self.TB)[level]

        def one(h, _):
            cols = jnp.concatenate([left[q, h * 2 + e].reshape(TOKENS, PAIR) for e in range(2)], axis=1)
            g = contract_first(cols, right[...]) * (1.0 / TOKENS**0.5)
            g = g.astype(jnp.bfloat16).reshape(2, 2, NC, PIECE, COLS)
            for part in range(PARTS):
                self.S[level, part, q, pl.ds(h * 2, 2)] = g[..., part * WIDTH : (part + 1) * WIDTH]
            return 0

        lax.fori_loop(0, CHUNK // 256, one, 0)

    def send_gradient(self, level, i, h):
        q = self.pair(i)
        for k, (dy, dc) in enumerate(PEERS):
            yy = lax.rem(self.y + dy, NY)
            cc = lax.rem(self.c + dc, NC)
            self.send(
                self.S.at[level, h, q, yy, :, cc],
                self.R.at[level, h, k, pl.ds(q * 2, 2)],
                self.yssem.at[level],
                self.yrsem.at[level, i, h],
                self.dev(dy=dy, dc=dc),
            )

    def wait_gradient(self, level, i, h):
        if (level, i, h) in self.came:
            return
        self.came.add((level, i, h))
        q = self.pair(i)
        self.wait(self.R.at[level, h, :, pl.ds(q * 2, 2)], self.yrsem.at[level, i, h])

    def passed(self, level, d, h, use):
        t = lax.rem(self.z + (d + NZ), NZ)
        q = lax.div(t, 2)
        low = lax.rem(t, 2)
        ids = [self.ch[self.path_of(), level]]
        ids += [self.ch[self.path_of(dy=-dy, dc=-dc), level] for dy, dc in PEERS]
        weight = [[jnp.where(i == m, 1.0, 0.0).astype(jnp.float32) for m in range(GRID)] for i in ids]

        def one(b, _):
            cols = pl.ds(pl.multiple_of(h * WIDTH + b * 128, 128), 128)
            place = pl.ds(pl.multiple_of(b * 128, 128), 128)
            parts = [self.S[level, h, q, self.y, low, self.c, :, place].astype(jnp.float32)]
            parts += [self.R[level, h, k, t, :, place].astype(jnp.float32) for k in range(NP)]
            for m in range(GRID):
                total = parts[0] * weight[0][m]
                for s in range(1, NP + 1):
                    total = total + parts[s] * weight[s][m]
                use(m, cols, place, total)
            return 0

        lax.fori_loop(0, WIDTH // 128, one, 0)

    def hop(self, level, d, h):
        self.wait_gradient(level, READY[d], h)
        slot = HOPS.index(d)
        up = d > 0
        k = abs(d)
        came = self.UP if up else self.DOWN
        if k < 4:
            self.wait(self.arriving(level, up, k, h), (self.usem if up else self.dsem).at[level, k, h])

        def use(m, cols, place, total):
            if k < 3 or k == 3 and (m < GRID // 2) == up:
                total = total + came[level, k, h, m, :, place].astype(jnp.float32)
            self.SB[level, slot, h, m, :, place] = total.astype(jnp.bfloat16)

        self.passed(level, d, h, use)
        sum_ref, ssem = self.SB.at[level, slot, h], self.zssem.at[level]
        if up:
            rows = pl.ds(0, GRID // 2 if k == 4 else GRID)
            self.send(sum_ref.at[rows], self.UP.at[level, k - 1, h, rows], ssem, self.usem.at[level, k - 1, h], self.dev(dz=1))
        if not up or k == 4:
            rows = pl.ds(GRID // 2, GRID // 2) if k == 4 else pl.ds(0, GRID)
            self.send(sum_ref.at[rows], self.DOWN.at[level, k - 1, h, rows], ssem, self.dsem.at[level, k - 1, h], self.dev(dz=-1))

    def arriving(self, level, up, k, h):
        half = GRID // 2
        buf = self.UP if up else self.DOWN
        if k == 3:
            return buf.at[level, 3, h, pl.ds(0 if up else half, half)]
        return buf.at[level, k, h]

    def counts(self):
        for level in range(2):

            def one(p, counts, level=level):
                i = self.ch[p, level]
                return tuple(n + jnp.where(i == m, 1, 0) for m, n in enumerate(counts))

            counts = lax.fori_loop(0, NY * NZ * NC, one, (jnp.int32(0),) * GRID)
            for m, n in enumerate(counts):
                n = jnp.full((8, 128), n, jnp.int32).astype(jnp.float32)
                self.INV[level, m] = 1.0 / jnp.maximum(n, 1.0)

    def own(self, level, h):
        self.wait_gradient(level, READY[0], h)
        if "momentum" not in self.came:
            self.came.add("momentum")
            self.wait(self.MOM, self.msem.at[0])
        self.wait(self.UP.at[level, 0, h], self.usem.at[level, 0, h])
        self.wait(self.DOWN.at[level, 0, h], self.dsem.at[level, 0, h])

        def use(m, cols, place, total):
            total = total + self.UP[level, 0, h, m, :, place].astype(jnp.float32)
            total = total + self.DOWN[level, 0, h, m, :, place].astype(jnp.float32)
            avg = total * self.INV[level, m, :1]
            mom = MU * self.MOM[level, m, :, cols] + avg
            self.NM[level, m, :, cols] = mom
            self.U[level][0][h, m, :, place] = (MU * mom + avg).astype(jnp.bfloat16)

        self.passed(level, 0, h, use)
        self.pass_on(level, 0, h)
        if h == PARTS - 1:
            pltpu.make_async_copy(self.NM.at[level], self.nm_hbm.at[level], self.msem.at[1 + level]).start()

    def pass_on(self, level, d, h):
        half = GRID // 2
        src = self.U[level][d % NZ].at[h]
        ssem = self.gssem.at[level]
        if d <= 0:
            to = self.U[level][(d - 1) % NZ].at[h]
            rows = pl.ds(0, half if d == -3 else GRID)
            self.send(src.at[rows], to.at[rows], ssem, self.gusem.at[level, 1 - d, h], self.dev(dz=1))
        if d >= 0:
            to = self.U[level][(d + 1) % NZ].at[h]
            rows = pl.ds(half, half) if d == 3 else pl.ds(0, GRID)
            self.send(src.at[rows], to.at[rows], ssem, self.gdsem.at[level, d + 1, h], self.dev(dz=-1))

    def spread(self, level, d, h):
        sem = self.gusem.at[level, -d, h] if d < 0 else self.gdsem.at[level, d, h]
        self.wait(self.U[level][d % NZ].at[h], sem)
        self.pass_on(level, d, h)

    def give(self, level, d):
        t = lax.rem(self.z + (d + NZ), NZ)
        rows = pl.ds(pl.multiple_of((self.y * NZ + t) * (NC * PIECE) + self.c * PIECE, PIECE), PIECE)
        buf = self.U[level][d % NZ]
        if d == 4:
            half = GRID // 2
            for h in range(PARTS):
                self.wait(buf.at[h, pl.ds(0, half)], self.gusem.at[level, 4, h])
                self.wait(buf.at[h, pl.ds(half, half)], self.gdsem.at[level, 4, h])
        dst = self.f_hbm[level].at[rows]
        for k, (dy, dc) in enumerate(PEERS + [(0, 0)]):
            m = self.ch[self.path_of(dy=dy, dc=dc), level]
            src = self.SEL.at[level, d % NZ, k]
            for h in range(PARTS):
                src[:, h * WIDTH : (h + 1) * WIDTH] = buf[h, m]
            if k < NP:
                self.send(src, dst, self.fssem.at[level], self.frsem.at[level], self.dev(dy=dy, dc=dc))
            else:
                pltpu.make_async_copy(src, dst, self.flsem.at[level]).start()

    def finish(self):
        for level in range(2):
            self.wait(self.f_hbm[level].at[pl.ds(0, D // 8 * 7)], self.frsem.at[level])
            self.wait(self.f_hbm[level].at[pl.ds(0, D // 8)], self.flsem.at[level])
            self.wait(self.SEL.at[level, :, pl.ds(0, NP)], self.fssem.at[level])
            self.wait(self.SB.at[level], self.zssem.at[level])
            self.wait(self.SB.at[level], self.gssem.at[level])
            self.wait(self.R.at[level], self.yssem.at[level])
            self.wait(self.T2[level].at[pl.ds(0, 3)], self.tssem.at[level])
            self.wait(self.NM.at[level], self.msem.at[1 + level])

    def run(self):
        self.came = set()
        self.barrier()
        for n in range(AHEAD):
            self.send_tokens(n)
        self.counts()
        for step, *args in SCHEDULE:
            getattr(self, step)(*args)
        self.finish()


SCRATCH = dict(
    X=pltpu.VMEM((NPAIR, NY, NX, TOK, PAIR), jnp.bfloat16),
    C=pltpu.VMEM((NPAIR, NY, NX, TOK, PAIR), jnp.bfloat16),
    W1=pltpu.VMEM((NPAIR, CHUNK, COLS), jnp.bfloat16),
    W2=pltpu.VMEM((NPAIR, CHUNK, COLS), jnp.bfloat16),
    ACC=pltpu.VMEM((TOKENS, COLS), jnp.float32),
    SL=pltpu.VMEM((TOKENS, COLS), jnp.float32),
    TB=pltpu.VMEM((TOKENS, COLS), jnp.bfloat16),
    DS=pltpu.VMEM((TOKENS, COLS), jnp.bfloat16),
    S=pltpu.VMEM((2, PARTS, NPAIR, NY, 2, NC, PIECE, WIDTH), jnp.bfloat16),
    R=pltpu.VMEM((2, PARTS, NP, NZ, PIECE, WIDTH), jnp.bfloat16),
    SB=pltpu.VMEM((2, len(HOPS), PARTS, GRID, PIECE, WIDTH), jnp.bfloat16),
    UP=pltpu.VMEM((2, 4, PARTS, GRID, PIECE, WIDTH), jnp.bfloat16),
    DOWN=pltpu.VMEM((2, 4, PARTS, GRID, PIECE, WIDTH), jnp.bfloat16),
    MOM=pltpu.VMEM((2, GRID, PIECE, COLS), jnp.float32),
    NM=pltpu.VMEM((2, GRID, PIECE, COLS), jnp.float32),
    INV=pltpu.VMEM((2, GRID, 8, 128), jnp.float32),
    SEL=pltpu.VMEM((2, NZ, NP + 1, PIECE, COLS), jnp.bfloat16),
    lsem=pltpu.SemaphoreType.DMA((2, NPAIR)),
    wsem=pltpu.SemaphoreType.DMA((2, NPAIR)),
    tssem=pltpu.SemaphoreType.DMA((2,)),
    trsem=pltpu.SemaphoreType.DMA((2, NPAIR, 3)),
    yssem=pltpu.SemaphoreType.DMA((2,)),
    yrsem=pltpu.SemaphoreType.DMA((2, NPAIR, PARTS)),
    zssem=pltpu.SemaphoreType.DMA((2,)),
    usem=pltpu.SemaphoreType.DMA((2, 4, PARTS)),
    dsem=pltpu.SemaphoreType.DMA((2, 4, PARTS)),
    gssem=pltpu.SemaphoreType.DMA((2,)),
    gusem=pltpu.SemaphoreType.DMA((2, 5, PARTS)),
    gdsem=pltpu.SemaphoreType.DMA((2, 5, PARTS)),
    fssem=pltpu.SemaphoreType.DMA((2,)),
    frsem=pltpu.SemaphoreType.DMA((2,)),
    flsem=pltpu.SemaphoreType.DMA((2,)),
    msem=pltpu.SemaphoreType.DMA((3,)),
)
UPDATES = [pltpu.VMEM((PARTS, GRID, PIECE, WIDTH), jnp.bfloat16)] * (2 * NZ)


def kernel(*refs):
    ins, outs, rest = refs[:6], refs[6:9], refs[9:]
    named = dict(zip(SCRATCH, rest))
    body = Body(ins, outs, named)
    updates = rest[len(SCRATCH) :]
    body.U = [updates[:NZ], updates[NZ:]]
    body.T2 = [body.X, body.C]
    body.run()


def sync(acts, cotan, first, second, choose, momentum):
    hbm = pl.BlockSpec(memory_space=pl.ANY)
    return pl.pallas_call(
        kernel,
        out_shape=(
            jax.ShapeDtypeStruct((D, COLS), jnp.bfloat16),
            jax.ShapeDtypeStruct((D, COLS), jnp.bfloat16),
            jax.ShapeDtypeStruct(momentum.shape, jnp.float32),
        ),
        in_specs=[hbm] * 4
        + [pl.BlockSpec(memory_space=pltpu.SMEM), hbm],
        out_specs=[hbm] * 3,
        scratch_shapes=list(SCRATCH.values()) + UPDATES,
        compiler_params=pltpu.CompilerParams(
            collective_id=0, has_side_effects=True, vmem_limit_bytes=58 * 2**20
        ),
        cost_estimate=pl.CostEstimate(flops=8 * 10**9, bytes_accessed=2 * 10**7, transcendentals=0),
    )(acts, cotan, first, second, choose, momentum)


def on_device(acts, cotan, w_in, w_out_t, choose, momentum):
    first, second = w_in[0], w_out_t[0]
    update_in, update_out, new_momentum = sync(acts, cotan, first, second, choose, momentum)

    def apply(weight, update):
        return (weight.astype(jnp.float32) - OUTER_LR * update.astype(jnp.float32)).astype(jnp.bfloat16)

    return (apply(first, update_in)[None], apply(second, update_out)[None], new_momentum)


def solution(mesh):
    return jax.shard_map(
        on_device,
        mesh=mesh,
        in_specs=(
            P(("path", "inner"), None),
            P(("path", "inner"), None),
            P("path", None, "inner"),
            P("path", None, "inner"),
            P(),
            P(None, None, "path", "inner"),
        ),
        out_specs=(
            P("path", None, "inner"),
            P("path", None, "inner"),
            P(None, None, "path", "inner"),
        ),
        check_vma=False,
    )
```

```python
import functools

import jax
import jax.numpy as jnp
from jax import lax
from jax.experimental import pallas as pl
from jax.experimental.pallas import tpu as pltpu
from jax.sharding import PartitionSpec as P

MU = 0.9
OUTER_LR = 0.7
MESH = pl.DeviceIdType.MESH

NX, NY, NZ, NC = 4, 4, 8, 2
GRID = 8
TOK = 256
TOKENS = TOK * NX
D = 2048
COLS = D // NX
PIECE = D // (NY * NZ * NC)
NPAIR = NZ // 2
PAIR = 2 * NC * PIECE
CHUNK = NY * PAIR
PEERS = [(2, 0), (2, 1), (1, 0), (1, 1), (3, 0), (3, 1), (0, 1)]
NP = len(PEERS)
ORDER = [[2, 2], [1, 3], [3, 1], [0, 0]]
AHEAD = 2
SCHEDULE = [
    ("forward_tokens", 0),
    ("forward_tokens", 1),
    ("product", 0, 0),
    ("forward_tokens", 2),
    ("product", 0, 1),
    ("forward_tokens", 3),
    ("product", 0, 2),
    ("forward_tokens", 4),
    ("product", 0, 3),
    ("activate",),
    ("forward_tokens", 5),
    ("product", 1, 0),
    ("gradient", 1, 0),
    ("send_gradient", 1, 0, 0),
    ("send_gradient", 1, 0, 1),
    ("forward_tokens", 6),
    ("hop", 1, 4, 0),
    ("gradient", 1, 1),
    ("send_gradient", 1, 1, 0),
    ("send_gradient", 1, 1, 1),
    ("product", 1, 1),
    ("hop", 1, 4, 1),
    ("hop", 1, -3, 0),
    ("forward_tokens", 7),
    ("hop", 1, 3, 0),
    ("hop", 1, 3, 1),
    ("gradient", 1, 2),
    ("send_gradient", 1, 2, 0),
    ("send_gradient", 1, 2, 1),
    ("hop", 1, -3, 1),
    ("product", 1, 2),
    ("gradient", 1, 3),
    ("send_gradient", 1, 3, 0),
    ("send_gradient", 1, 3, 1),
    ("hop", 1, 2, 0),
    ("hop", 1, -2, 0),
    ("product", 1, 3),
    ("slope",),
    ("gradient", 0, 2),
    ("hop", 1, 2, 1),
    ("hop", 1, -2, 1),
    ("gradient", 0, 0),
    ("send_gradient", 0, 0, 0),
    ("send_gradient", 0, 0, 1),
    ("hop", 1, 1, 0),
    ("hop", 1, -1, 0),
    ("gradient", 0, 1),
    ("send_gradient", 0, 1, 1),
    ("send_gradient", 0, 1, 0),
    ("hop", 1, 1, 1),
    ("hop", 1, -1, 1),
    ("gradient", 0, 3),
    ("send_gradient", 0, 3, 1),
    ("send_gradient", 0, 3, 0),
    ("hop", 0, 4, 0),
    ("send_gradient", 0, 2, 0),
    ("own", 1, 0),
    ("send_gradient", 0, 2, 1),
    ("hop", 0, 4, 1),
    ("own", 1, 1),
    ("give", 1, 0),
    ("spread", 1, -1, 0),
    ("spread", 1, 1, 0),
    ("hop", 0, 3, 1),
    ("hop", 0, 3, 0),
    ("hop", 0, -3, 0),
    ("hop", 0, -3, 1),
    ("spread", 1, -1, 1),
    ("give", 1, -1),
    ("spread", 1, 1, 1),
    ("give", 1, 1),
    ("spread", 1, -2, 0),
    ("spread", 1, 2, 0),
    ("hop", 0, -2, 0),
    ("hop", 0, 2, 0),
    ("hop", 0, 2, 1),
    ("hop", 0, -2, 1),
    ("spread", 1, -2, 1),
    ("give", 1, -2),
    ("spread", 1, 2, 1),
    ("give", 1, 2),
    ("spread", 1, -3, 0),
    ("spread", 1, 3, 0),
    ("hop", 0, 1, 0),
    ("hop", 0, -1, 0),
    ("hop", 0, 1, 1),
    ("hop", 0, -1, 1),
    ("spread", 1, -3, 1),
    ("spread", 1, 3, 1),
    ("give", 1, 3),
    ("give", 1, -3),
    ("own", 0, 0),
    ("own", 0, 1),
    ("give", 0, 0),
    ("give", 1, 4),
    ("spread", 0, -1, 0),
    ("spread", 0, 1, 0),
    ("spread", 0, -1, 1),
    ("give", 0, -1),
    ("spread", 0, 1, 1),
    ("give", 0, 1),
    ("spread", 0, -2, 0),
    ("spread", 0, 2, 0),
    ("spread", 0, -2, 1),
    ("give", 0, -2),
    ("spread", 0, 2, 1),
    ("give", 0, 2),
    ("spread", 0, -3, 0),
    ("spread", 0, 3, 0),
    ("spread", 0, -3, 1),
    ("give", 0, -3),
    ("spread", 0, 3, 1),
    ("give", 0, 3),
    ("give", 0, 4),
]
HOPS = [4, 3, 2, 1, -3, -2, -1]
READY = {4: 0, 3: 1, -3: 1, 2: 2, -2: 2, 1: 3, -1: 3, 0: 3}
PARTS = 2
WIDTH = COLS // PARTS


def contract_first(left, right):
    return lax.dot_general(
        left, right, (((0,), (0,)), ((), ())), preferred_element_type=jnp.float32
    )


class Body:
    def __init__(self, ins, outs, scratch):
        self.x_hbm, self.c_hbm, self.w1_hbm, self.w2_hbm, self.ch, self.mom_hbm = ins
        self.f_hbm = outs[:2]
        self.nm_hbm = outs[2]
        for name, ref in scratch.items():
            setattr(self, name, ref)
        path = lax.axis_index("path")
        self.x = lax.axis_index("inner")
        self.y = lax.div(path, NZ * NC)
        self.z = lax.rem(lax.div(path, NC), NZ)
        self.c = lax.rem(path, NC)
        self.zp = lax.div(self.z, 2)

    def path_of(self, dy=0, dz=0, dc=0):
        y = lax.rem(self.y + (dy + NY), NY)
        z = lax.rem(self.z + (dz + NZ), NZ)
        c = lax.rem(self.c + (dc + NC), NC)
        return (y * NZ + z) * NC + c

    def dev(self, dy=0, dz=0, dc=0, dx=0):
        return (self.path_of(dy, dz, dc), lax.rem(self.x + (dx + NX), NX))

    def send(self, src, dst, ssem, rsem, dev):
        pltpu.make_async_remote_copy(
            src_ref=src, dst_ref=dst, send_sem=ssem, recv_sem=rsem, device_id=dev, device_id_type=MESH
        ).start()

    def wait(self, ref, sem):
        pltpu.make_async_copy(ref, ref, sem).wait()

    def barrier(self):
        bar = pltpu.get_barrier_semaphore()
        partners = [self.dev(dx=1), self.dev(dx=-1)]
        partners += [self.dev(dy=dy, dc=dc) for dy, dc in PEERS]
        partners += [self.dev(dz=1), self.dev(dz=-1)]
        for partner in partners:
            pl.semaphore_signal(bar, inc=1, device_id=partner, device_id_type=MESH)
        self.load_local()
        pl.semaphore_wait(bar, len(partners))

    def pair(self, i):
        even, odd = ORDER[i]
        return lax.rem(self.zp + even + (odd - even) * lax.rem(self.z, 2) + NPAIR, NPAIR)

    def load_local(self):
        for a, (hbm, whbm, wbuf) in enumerate(
            ((self.x_hbm, self.w1_hbm, self.W1), (self.c_hbm, self.w2_hbm, self.W2))
        ):
            for i in range(NPAIR):
                q = self.pair(i)

                def tokens(yy, _, a=a, i=i, q=q, hbm=hbm):
                    cols = pl.multiple_of(yy * (NPAIR * PAIR) + q * PAIR, PAIR)
                    pltpu.make_async_copy(
                        hbm.at[:, pl.ds(cols, PAIR)], self.T2[a].at[q, yy, self.x], self.lsem.at[a, i]
                    ).start()
                    return 0

                lax.fori_loop(0, NY, tokens, 0)
            for i in range(NPAIR):
                q = self.pair(i)

                def weights(yy, _, a=a, i=i, q=q, whbm=whbm, wbuf=wbuf):
                    rows = pl.multiple_of(yy * (NPAIR * PAIR) + q * PAIR, PAIR)
                    place = pl.multiple_of(yy * PAIR, PAIR)
                    pltpu.make_async_copy(
                        whbm.at[pl.ds(rows, PAIR)], wbuf.at[q, pl.ds(place, PAIR)], self.wsem.at[a, i]
                    ).start()
                    return 0

                lax.fori_loop(0, NY, weights, 0)
        pltpu.make_async_copy(self.mom_hbm, self.MOM, self.msem.at[0]).start()

    def send_tokens(self, n):
        a, i = divmod(n, NPAIR)
        own = self.T2[a].at[self.pair(i), :, self.x]
        self.wait(own, self.lsem.at[a, i])
        for k, dx in enumerate((1, -1)):
            self.send(own, own, self.tssem.at[a], self.trsem.at[a, i, k], self.dev(dx=dx))

    def forward_tokens(self, n):
        a, i = divmod(n, NPAIR)
        q = self.pair(i)
        for k, dx in enumerate((1, -1)):
            src = lax.rem(self.x + (NX - dx), NX)
            self.wait(self.T2[a].at[q, :, src], self.trsem.at[a, i, k])
            half = self.T2[a].at[q, pl.ds(k * (NY // 2), NY // 2), src]
            self.send(half, half, self.tssem.at[a], self.trsem.at[a, i, 2], self.dev(dx=dx))
        if n + AHEAD < 2 * NPAIR:
            self.send_tokens(n + AHEAD)

    def wait_tokens(self, n):
        if n in self.came:
            return
        self.came.add(n)
        a, i = divmod(n, NPAIR)
        q = self.pair(i)
        self.wait((self.W1, self.W2)[a].at[q], self.wsem.at[a, i])
        self.wait(self.T2[a].at[q, :, lax.rem(self.x + 2, NX)], self.trsem.at[a, i, 2])

    def product(self, a, i):
        self.wait_tokens(a * NPAIR + i)
        q = self.pair(i)
        wbuf = (self.W1, self.W2)[a]

        def one(h, _):
            rows = pl.ds(pl.multiple_of(h * 512, 512), 512)
            left = jnp.concatenate(
                [self.T2[a][q, yy, pl.ds(h * 2, 2)].reshape(512, PAIR) for yy in range(NY)], axis=1
            )
            part = jnp.dot(left, wbuf[q], preferred_element_type=jnp.float32)
            if i == 0:
                self.ACC[rows] = part
            else:
                self.ACC[rows] = self.ACC[rows] + part
            return 0

        lax.fori_loop(0, TOKENS // 512, one, 0)

    def activate(self):
        def one(h, _):
            rows = pl.ds(pl.multiple_of(h * 64, 64), 64)
            t = jnp.tanh(self.ACC[rows])
            self.TB[rows] = t.astype(jnp.bfloat16)
            self.SL[rows] = 1.0 - t * t
            return 0

        lax.fori_loop(0, TOKENS // 64, one, 0)

    def slope(self):
        def one(h, _):
            rows = pl.ds(pl.multiple_of(h * 64, 64), 64)
            self.DS[rows] = (self.ACC[rows] * self.SL[rows]).astype(jnp.bfloat16)
            return 0

        lax.fori_loop(0, TOKENS // 64, one, 0)

    def gradient(self, level, i):
        if level == 1:
            self.wait_tokens(NPAIR + i)
        q = self.pair(i)
        left = self.T2[level]
        right = (self.DS, self.TB)[level]

        def one(h, _):
            cols = jnp.concatenate([left[q, h * 2 + e].reshape(TOKENS, PAIR) for e in range(2)], axis=1)
            g = contract_first(cols, right[...]) * (1.0 / TOKENS**0.5)
            g = g.astype(jnp.bfloat16).reshape(2, 2, NC, PIECE, COLS)
            for part in range(PARTS):
                self.S[level, part, q, pl.ds(h * 2, 2)] = g[..., part * WIDTH : (part + 1) * WIDTH]
            return 0

        lax.fori_loop(0, CHUNK // 256, one, 0)

    def send_gradient(self, level, i, h):
        q = self.pair(i)
        for k, (dy, dc) in enumerate(PEERS):
            yy = lax.rem(self.y + dy, NY)
            cc = lax.rem(self.c + dc, NC)
            self.send(
                self.S.at[level, h, q, yy, :, cc],
                self.R.at[level, h, k, pl.ds(q * 2, 2)],
                self.yssem.at[level],
                self.yrsem.at[level, i, h],
                self.dev(dy=dy, dc=dc),
            )

    def wait_gradient(self, level, last, h):
        for i in range(last + 1):
            if (level, i, h) not in self.came:
                self.came.add((level, i, h))
                self.wait(self.R.at[level, h, :, pl.ds(self.pair(i) * 2, 2)], self.yrsem.at[level, i, h])

    def passed(self, level, d, h, use):
        t = lax.rem(self.z + (d + NZ), NZ)
        q = lax.div(t, 2)
        low = lax.rem(t, 2)
        ids = [self.ch[level, self.path_of()]]
        ids += [self.ch[level, self.path_of(dy=-dy, dc=-dc)] for dy, dc in PEERS]
        weight = [[jnp.where(i == m, 1.0, 0.0).astype(jnp.float32) for m in range(GRID)] for i in ids]

        def one(b, _):
            cols = pl.ds(pl.multiple_of(h * WIDTH + b * 128, 128), 128)
            place = pl.ds(pl.multiple_of(b * 128, 128), 128)
            parts = [self.S[level, h, q, self.y, low, self.c, :, place].astype(jnp.float32)]
            parts += [self.R[level, h, k, t, :, place].astype(jnp.float32) for k in range(NP)]
            for m in range(GRID):
                total = parts[0] * weight[0][m]
                for s in range(1, NP + 1):
                    total = total + parts[s] * weight[s][m]
                use(m, cols, place, total)
            return 0

        lax.fori_loop(0, WIDTH // 128, one, 0)

    def hop(self, level, d, h):
        self.wait_gradient(level, READY[d], h)
        slot = HOPS.index(d)
        up = d > 0
        k = abs(d)
        came = self.UP if up else self.DOWN
        if k < 4:
            self.wait(self.arriving(level, up, k, h), (self.usem if up else self.dsem).at[level, k, h])

        def use(m, cols, place, total):
            if k < 3 or k == 3 and (m < GRID // 2) == up:
                total = total + came[level, k, h, m, :, place].astype(jnp.float32)
            self.SB[level, slot, h, m, :, place] = total.astype(jnp.bfloat16)

        self.passed(level, d, h, use)
        sum_ref, ssem = self.SB.at[level, slot, h], self.zssem.at[level]
        if up:
            rows = pl.ds(0, GRID // 2 if k == 4 else GRID)
            self.send(sum_ref.at[rows], self.UP.at[level, k - 1, h, rows], ssem, self.usem.at[level, k - 1, h], self.dev(dz=1))
        if not up or k == 4:
            rows = pl.ds(GRID // 2, GRID // 2) if k == 4 else pl.ds(0, GRID)
            self.send(sum_ref.at[rows], self.DOWN.at[level, k - 1, h, rows], ssem, self.dsem.at[level, k - 1, h], self.dev(dz=-1))

    def arriving(self, level, up, k, h):
        half = GRID // 2
        buf = self.UP if up else self.DOWN
        if k == 3:
            return buf.at[level, 3, h, pl.ds(0 if up else half, half)]
        return buf.at[level, k, h]

    def counts(self):
        for level in range(2):

            def one(p, counts, level=level):
                i = self.ch[level, p]
                return tuple(n + jnp.where(i == m, 1, 0) for m, n in enumerate(counts))

            counts = lax.fori_loop(0, NY * NZ * NC, one, (jnp.int32(0),) * GRID)
            for m, n in enumerate(counts):
                n = jnp.full((8, 128), n, jnp.int32).astype(jnp.float32)
                self.INV[level, m] = 1.0 / jnp.maximum(n, 1.0)

    def own(self, level, h):
        self.wait_gradient(level, READY[0], h)
        if "momentum" not in self.came:
            self.came.add("momentum")
            self.wait(self.MOM, self.msem.at[0])
        self.wait(self.UP.at[level, 0, h], self.usem.at[level, 0, h])
        self.wait(self.DOWN.at[level, 0, h], self.dsem.at[level, 0, h])

        def use(m, cols, place, total):
            total = total + self.UP[level, 0, h, m, :, place].astype(jnp.float32)
            total = total + self.DOWN[level, 0, h, m, :, place].astype(jnp.float32)
            avg = total * self.INV[level, m, :1]
            mom = MU * self.MOM[level, m, :, cols] + avg
            self.NM[level, m, :, cols] = mom
            self.U[level][0][h, m, :, place] = (MU * mom + avg).astype(jnp.bfloat16)

        self.passed(level, 0, h, use)
        self.pass_on(level, 0, h)
        if h == PARTS - 1:
            pltpu.make_async_copy(self.NM.at[level], self.nm_hbm.at[level], self.msem.at[1 + level]).start()

    def pass_on(self, level, d, h):
        half = GRID // 2
        src = self.U[level][d % NZ].at[h]
        ssem = self.gssem.at[level]
        if d <= 0:
            to = self.U[level][(d - 1) % NZ].at[h]
            rows = pl.ds(0, half if d == -3 else GRID)
            self.send(src.at[rows], to.at[rows], ssem, self.gusem.at[level, 1 - d, h], self.dev(dz=1))
        if d >= 0:
            to = self.U[level][(d + 1) % NZ].at[h]
            rows = pl.ds(half, half) if d == 3 else pl.ds(0, GRID)
            self.send(src.at[rows], to.at[rows], ssem, self.gdsem.at[level, d + 1, h], self.dev(dz=-1))

    def spread(self, level, d, h):
        sem = self.gusem.at[level, -d, h] if d < 0 else self.gdsem.at[level, d, h]
        self.wait(self.U[level][d % NZ].at[h], sem)
        self.pass_on(level, d, h)

    def give(self, level, d):
        t = lax.rem(self.z + (d + NZ), NZ)
        rows = pl.ds(pl.multiple_of((self.y * NZ + t) * (NC * PIECE) + self.c * PIECE, PIECE), PIECE)
        buf = self.U[level][d % NZ]
        if d == 4:
            half = GRID // 2
            for h in range(PARTS):
                self.wait(buf.at[h, pl.ds(0, half)], self.gusem.at[level, 4, h])
                self.wait(buf.at[h, pl.ds(half, half)], self.gdsem.at[level, 4, h])
        dst = self.f_hbm[level].at[rows]
        for k, (dy, dc) in enumerate(PEERS + [(0, 0)]):
            m = self.ch[level, self.path_of(dy=dy, dc=dc)]
            src = self.SEL.at[level, d % NZ, k]
            for h in range(PARTS):
                src[:, h * WIDTH : (h + 1) * WIDTH] = buf[h, m]
            if k < NP:
                self.send(src, dst, self.fssem.at[level], self.frsem.at[level], self.dev(dy=dy, dc=dc))
            else:
                pltpu.make_async_copy(src, dst, self.flsem.at[level]).start()

    def finish(self):
        for level in range(2):
            self.wait(self.f_hbm[level].at[pl.ds(0, D // 8 * 7)], self.frsem.at[level])
            self.wait(self.f_hbm[level].at[pl.ds(0, D // 8)], self.flsem.at[level])
            self.wait(self.SEL.at[level, :, pl.ds(0, NP)], self.fssem.at[level])
            self.wait(self.SB.at[level], self.zssem.at[level])
            self.wait(self.SB.at[level], self.gssem.at[level])
            self.wait(self.R.at[level], self.yssem.at[level])
            self.wait(self.T2[level].at[pl.ds(0, 3)], self.tssem.at[level])
            self.wait(self.NM.at[level], self.msem.at[1 + level])

    def run(self):
        self.came = set()
        self.barrier()
        for n in range(AHEAD):
            self.send_tokens(n)
        self.counts()
        for step, *args in SCHEDULE:
            getattr(self, step)(*args)
        self.finish()


SCRATCH = dict(
    X=pltpu.VMEM((NPAIR, NY, NX, TOK, PAIR), jnp.bfloat16),
    C=pltpu.VMEM((NPAIR, NY, NX, TOK, PAIR), jnp.bfloat16),
    W1=pltpu.VMEM((NPAIR, CHUNK, COLS), jnp.bfloat16),
    W2=pltpu.VMEM((NPAIR, CHUNK, COLS), jnp.bfloat16),
    ACC=pltpu.VMEM((TOKENS, COLS), jnp.float32),
    SL=pltpu.VMEM((TOKENS, COLS), jnp.float32),
    TB=pltpu.VMEM((TOKENS, COLS), jnp.bfloat16),
    DS=pltpu.VMEM((TOKENS, COLS), jnp.bfloat16),
    S=pltpu.VMEM((2, PARTS, NPAIR, NY, 2, NC, PIECE, WIDTH), jnp.bfloat16),
    R=pltpu.VMEM((2, PARTS, NP, NZ, PIECE, WIDTH), jnp.bfloat16),
    SB=pltpu.VMEM((2, len(HOPS), PARTS, GRID, PIECE, WIDTH), jnp.bfloat16),
    UP=pltpu.VMEM((2, 4, PARTS, GRID, PIECE, WIDTH), jnp.bfloat16),
    DOWN=pltpu.VMEM((2, 4, PARTS, GRID, PIECE, WIDTH), jnp.bfloat16),
    MOM=pltpu.VMEM((2, GRID, PIECE, COLS), jnp.float32),
    NM=pltpu.VMEM((2, GRID, PIECE, COLS), jnp.float32),
    INV=pltpu.VMEM((2, GRID, 8, 128), jnp.float32),
    SEL=pltpu.VMEM((2, NZ, NP + 1, PIECE, COLS), jnp.bfloat16),
    lsem=pltpu.SemaphoreType.DMA((2, NPAIR)),
    wsem=pltpu.SemaphoreType.DMA((2, NPAIR)),
    tssem=pltpu.SemaphoreType.DMA((2,)),
    trsem=pltpu.SemaphoreType.DMA((2, NPAIR, 3)),
    yssem=pltpu.SemaphoreType.DMA((2,)),
    yrsem=pltpu.SemaphoreType.DMA((2, NPAIR, PARTS)),
    zssem=pltpu.SemaphoreType.DMA((2,)),
    usem=pltpu.SemaphoreType.DMA((2, 4, PARTS)),
    dsem=pltpu.SemaphoreType.DMA((2, 4, PARTS)),
    gssem=pltpu.SemaphoreType.DMA((2,)),
    gusem=pltpu.SemaphoreType.DMA((2, 5, PARTS)),
    gdsem=pltpu.SemaphoreType.DMA((2, 5, PARTS)),
    fssem=pltpu.SemaphoreType.DMA((2,)),
    frsem=pltpu.SemaphoreType.DMA((2,)),
    flsem=pltpu.SemaphoreType.DMA((2,)),
    msem=pltpu.SemaphoreType.DMA((3,)),
)
UPDATES = [pltpu.VMEM((PARTS, GRID, PIECE, WIDTH), jnp.bfloat16)] * (2 * NZ)


def kernel(*refs):
    ins, outs, rest = refs[:6], refs[6:9], refs[9:]
    named = dict(zip(SCRATCH, rest))
    body = Body(ins, outs, named)
    updates = rest[len(SCRATCH) :]
    body.U = [updates[:NZ], updates[NZ:]]
    body.T2 = [body.X, body.C]
    body.run()


def sync(acts, cotan, first, second, choose, momentum):
    hbm = pl.BlockSpec(memory_space=pl.ANY)
    return pl.pallas_call(
        kernel,
        out_shape=(
            jax.ShapeDtypeStruct((D, COLS), jnp.bfloat16),
            jax.ShapeDtypeStruct((D, COLS), jnp.bfloat16),
            jax.ShapeDtypeStruct(momentum.shape, jnp.float32),
        ),
        in_specs=[hbm] * 4
        + [pl.BlockSpec(memory_space=pltpu.SMEM), hbm],
        out_specs=[hbm] * 3,
        scratch_shapes=list(SCRATCH.values()) + UPDATES,
        compiler_params=pltpu.CompilerParams(
            collective_id=0, has_side_effects=True, vmem_limit_bytes=58 * 2**20
        ),
        cost_estimate=pl.CostEstimate(flops=8 * 10**9, bytes_accessed=2 * 10**7, transcendentals=0),
    )(acts, cotan, first, second, choose.T, momentum)


BLOCKS = 4
ROWS = D // BLOCKS


def step_kernel(w1, w2, f1, f2, nm, o1, o2, nm_out, weight, update, result, mom, wsem, fsem, osem, msem):
    pieces = [(level, b) for b in range(BLOCKS) for level in range(2)]

    def load(level, b):
        rows = pl.ds(b * ROWS, ROWS)
        return (
            pltpu.make_async_copy((w1, w2)[level].at[rows], weight.at[level, rows], wsem.at[level, b]),
            pltpu.make_async_copy((f1, f2)[level].at[rows], update.at[level, rows], fsem.at[level, b]),
        )

    def store(level, b):
        rows = pl.ds(b * ROWS, ROWS)
        return pltpu.make_async_copy(result.at[level, rows], (o1, o2)[level].at[rows], osem.at[level, b])

    for piece in pieces:
        for copy in load(*piece):
            copy.start()
    pltpu.make_async_copy(nm, mom, msem).start()
    for level, b in pieces:
        for copy in load(level, b):
            copy.wait()

        def one(i, _, level=level, b=b):
            rows = pl.ds(pl.multiple_of(b * ROWS + i * 64, 64), 64)
            new = weight[level, rows].astype(jnp.float32) - OUTER_LR * update[level, rows].astype(jnp.float32)
            result[level, rows] = new.astype(jnp.bfloat16)
            return 0

        lax.fori_loop(0, ROWS // 64, one, 0)
        store(level, b).start()
    pltpu.make_async_copy(nm, mom, msem).wait()
    last = pltpu.make_async_copy(mom, nm_out, msem)
    last.start()
    for piece in pieces:
        store(*piece).wait()
    last.wait()


def outer_step(first, second, update_in, update_out, new_momentum):
    hbm = pl.BlockSpec(memory_space=pl.ANY)
    whole = pltpu.VMEM((2, D, COLS), jnp.bfloat16)
    sems = pltpu.SemaphoreType.DMA((2, BLOCKS))
    return pl.pallas_call(
        step_kernel,
        out_shape=tuple(jax.ShapeDtypeStruct(a.shape, a.dtype) for a in (first, second, new_momentum)),
        in_specs=[hbm] * 5,
        out_specs=[hbm] * 3,
        scratch_shapes=[whole, whole, whole, pltpu.VMEM(new_momentum.shape, jnp.float32), sems, sems, sems, pltpu.SemaphoreType.DMA],
        compiler_params=pltpu.CompilerParams(vmem_limit_bytes=59 * 2**20),
        cost_estimate=pl.CostEstimate(flops=4 * 10**6, bytes_accessed=14 * 2**20, transcendentals=0),
    )(first, second, update_in, update_out, new_momentum)


def on_device(acts, cotan, w_in, w_out_t, choose, momentum):
    first, second = w_in[0], w_out_t[0]
    updates = sync(acts, cotan, first, second, choose, momentum)
    new_in, new_out_t, new_momentum = outer_step(first, second, *updates)
    return (new_in[None], new_out_t[None], new_momentum)


def solution(mesh):
    return jax.shard_map(
        on_device,
        mesh=mesh,
        in_specs=(
            P(("path", "inner"), None),
            P(("path", "inner"), None),
            P("path", None, "inner"),
            P("path", None, "inner"),
            P(),
            P(None, None, "path", "inner"),
        ),
        out_specs=(
            P("path", None, "inner"),
            P("path", None, "inner"),
            P(None, None, "path", "inner"),
        ),
        check_vma=False,
    )
```
